1024 devices in a mesh: dp: 16 (over z, core), expert: 64 (over x, y).
Axes of the slice: x: 8, y: 8, z: 8, core: 2. Of those that a mesh axis runs over, the one named last changes fastest.
Arguments:
- expert_ids: int32 [16384, 8], P(('dp', 'expert')), may hold values from 0 to 63, all different within a row; in each aligned block of 16 rows (0 to 15, 16 to 31, ...) at most 3 rows name the same one
- grad_hidden: bfloat16 [16384, 8, 768], P(('dp', 'expert')), may hold values from -1.796875 to 1.796875
- stored_inputs: bfloat16 [16, 64, 64, 3, 2048], P('dp', 'expert'), may hold values from -6 to 6
- gate_weight: bfloat16 [64, 2048, 768], P('expert'), may hold values from -0.125 to 0.125
- up_weight: bfloat16 [64, 2048, 768], P('expert'), may hold values from -0.125 to 0.125
Outputs:
- grad_tokens: bfloat16 [16384, 2048], P(('dp', 'expert'))
- grad_gate: float32 [64, 2048, 768], P('expert', 'dp')
The draws below stay inside these ranges and needn't reach their ends.
Inputs may be any that keep to these rules, and one draw needn't show every extreme that they name: `expert_ids`: among the 16 tokens of one device no expert is named more than 3 times, and in every draw some device names some expert exactly 3 times; a token names 8 different experts.
All inputs are finite; a program needn't handle non-finite values.
Results may differ from the reference program's by a relative error of at most 0.02.
Values may be sent and summed in bfloat16 or wider, within the bound.
No kernel may reach another device: no remote copies, remote signals or barrier semaphores. Data moves between devices by JAX's collectives and lax.ppermute only.
A program may use at most 64 MiB of HBM per device.

```python
import math
import jax
import jax.numpy as jnp
import numpy as np
from jax import lax

D = 2048
FF = 768
TOP = 8
TOK_DEV = 16
EXPERTS = 64
CAP = 3
TOKENS = 16384
N_DP = 16
N_EXPERT = 64


def strengthened(result, rng, source, target, parts, factor):
    owner, partner = [(jnp.arange(result.shape[axis_at]) // (result.shape[axis_at] // parts)).reshape([-1 if axis == axis_at else 1 for axis in range(result.ndim)]) for axis_at in (source, target)]
    chosen = jax.random.permutation(rng, parts)[partner]
    strong = (owner == chosen) | (owner == (partner + parts // 2) % parts)
    return jnp.where(strong, factor * result, result)


def levels(key, shape, pieces, low, top_value):
    factor_of = 1.0
    for dim, parts in pieces:
        steps = jax.random.uniform(jax.random.fold_in(jax.random.fold_in(key, 6), dim), (parts,), jnp.float32, low / len(pieces), top_value / len(pieces))
        factor_of = factor_of * jnp.repeat(jnp.exp(steps), shape[dim] // parts).reshape((-1,) + (1,) * (len(shape) - 1 - dim))
    return factor_of


def routed_block(rng, own, number, rows, amount, top, bound, slope):
    order = jax.random.permutation(rng, amount)
    packed, common = shares(amount, rows * top, bound, slope, True), shares(amount, rows * top, bound, slope, False)
    places = jnp.arange(amount)

    def named(tallies, rotation):
        used = int((tallies > 0).sum())
        fixed = max(1, used // 4)
        shifted = fixed + (places - fixed + rotation * (used - fixed)) % max(1, amount - fixed)
        return jnp.zeros((amount,), jnp.int32).at[order[jnp.where(places < fixed, places, shifted)]].set(jnp.asarray(tallies, jnp.int32))

    tallies = jnp.where(number % 4 == 0, named(packed, number // 4), named(common, number - number // 4 - 1))
    mixed = jax.random.permutation(jax.random.fold_in(own, 3), amount)
    source_of, sink = mixed[0:amount // 2 * 2:2], mixed[1:amount // 2 * 2:2]
    room = jnp.minimum(tallies[source_of] - 1, bound - tallies[sink]) // 2
    room = jnp.where((source_of == order[0]) | (sink == order[0]) | (tallies[sink] == 0), 0, jnp.maximum(room, 0))
    shifted = jax.random.randint(jax.random.fold_in(own, 4), (amount // 2,), 0, 1 << 20) % (room + 1)
    tallies = tallies.at[source_of].add(-shifted).at[sink].add(shifted)
    members = jnp.searchsorted(jnp.cumsum(tallies), jnp.arange(rows * top), side="right").astype(jnp.int32)
    table = members.reshape(top, rows).T
    table = table[jax.random.permutation(jax.random.fold_in(own, 1), rows)]
    rotation = jax.random.randint(jax.random.fold_in(own, 2), (rows, 1), 0, top)
    return jnp.take_along_axis(table, (jnp.arange(top)[None, :] + rotation) % top, axis=1)


def shares(amount, total, bound, lean, full):
    weights = [(1 << 20) // math.isqrt(standing ** lean) + 1 for standing in range(1, amount + 1)]
    largest = bound if full else min(bound, max(-(-total // amount), total * weights[0] // sum(weights)))
    least = 1 if total - largest >= amount - 1 else 0
    holding, rest = [largest] + [least] * (amount - 1), total - largest - least * (amount - 1)
    while rest > 0:
        free = [i for i in range(1, amount) if holding[i] < largest] or [i for i in range(1, amount) if holding[i] < bound]
        pool, budget = sum([weights[i] for i in free]), rest
        for i in free:
            extra = min(bound - holding[i], max(1, budget * weights[i] // pool), rest)
            holding[i] = holding[i] + extra
            rest = rest - extra
    return np.array(holding)


def gaussian(stream_key, shape, deviation, bound, shards=(), held_as=jnp.bfloat16):
    drawn = jax.random.normal(stream_key, shape, jnp.float32) * deviation
    if len(shards) > 0:
        drawn = levels(stream_key, shape, shards, -0.22, 0.18) * drawn
    return jnp.clip(drawn, min=-bound, max=bound).astype(held_as)


def heavy_noise(rng, shape, width, limit, shards, heavy, kind=jnp.bfloat16):
    drawn = width * jax.random.normal(rng, shape, jnp.float32)
    if shards:
        drawn = drawn * levels(rng, shape, shards, -0.22, 0.18)
    return jnp.clip(strengthened(drawn, jax.random.fold_in(rng, 3), *heavy), -limit, limit).astype(kind)


def setup_inputs(seed: int = 0) -> dict:
    keys = jax.random.split(jax.random.key(seed), 6)
    expert_ids_keys = jax.random.split(jax.random.fold_in(keys[0], 1), TOKENS // TOK_DEV)
    expert_ids_turns = jax.random.permutation(jax.random.fold_in(keys[0], 3), TOKENS // TOK_DEV)
    expert_ids = jax.vmap(lambda own, number: routed_block(jax.random.fold_in(keys[0], 2), own, number, TOK_DEV, EXPERTS, TOP, CAP, 2))(expert_ids_keys, expert_ids_turns).reshape((TOKENS, TOP))
    grad_hidden = gaussian(keys[1], (TOKENS, TOP, FF), 0.3, 1.796875, ((0, 1024),))
    stored_inputs = heavy_noise(keys[2], (N_DP, EXPERTS, N_EXPERT, CAP, D), 1.0, 6.0, ((0, 16), (1, 64)), (0, 4, 16, 2.0))
    gate_weight = gaussian(keys[3], (EXPERTS, D, FF), D ** -0.5, 0.125, ((0, 64),))
    up_weight = gaussian(keys[4], (EXPERTS, D, FF), D ** -0.5, 0.125, ((0, 64),))
    return {"expert_ids": expert_ids, "grad_hidden": grad_hidden, "stored_inputs": stored_inputs, "gate_weight": gate_weight, "up_weight": up_weight}


def expert_gradient_pass(x_rows, dh_rows, wg, wu):
    gate = jnp.dot(x_rows, wg, preferred_element_type=jnp.float32)
    up = jnp.dot(x_rows, wu, preferred_element_type=jnp.float32)
    sig = jax.nn.sigmoid(gate)
    dh_wide = dh_rows.astype(jnp.float32)
    dgate = (dh_wide * up * sig * (1.0 + gate * (1.0 - sig))).astype(jnp.bfloat16)
    dup = (dh_wide * gate * sig).astype(jnp.bfloat16)
    dims = (((1,), (1,)), ((), ()))
    back = lax.dot_general(dgate, wg, dims, preferred_element_type=jnp.float32)
    back = back + lax.dot_general(dup, wu, dims, preferred_element_type=jnp.float32)
    return dgate, back.astype(jnp.bfloat16)


def replica_sum(input_split, gradient_list):
    part_list = jnp.einsum("gan,gal->gnl", input_split, gradient_list.astype(jnp.float32)).astype(jnp.bfloat16)
    part_list = lax.optimization_barrier(part_list)
    return jnp.sum(part_list.astype(jnp.float32), axis=0)


def reference(expert_ids, grad_hidden, stored_inputs, gate_weight, up_weight):
    block_list = N_DP * N_EXPERT
    per_block = TOK_DEV * TOP
    ids = expert_ids.reshape(block_list, per_block).astype(jnp.int32)
    onehot = (ids[:, :, None] == jnp.arange(EXPERTS, dtype=jnp.int32)[None, None, :]).astype(jnp.int32)
    rank = jnp.cumsum(onehot, axis=1) - onehot
    slot = jnp.sum(rank * onehot, axis=2).astype(jnp.int32)
    block_ids = jnp.broadcast_to(jnp.arange(block_list, dtype=jnp.int32)[:, None], (block_list, per_block))
    replica = (block_ids // N_EXPERT).astype(jnp.int32)
    sender_index = (block_ids % N_EXPERT).astype(jnp.int32)
    arrived = jnp.zeros((N_DP, EXPERTS, N_EXPERT, CAP, FF), grad_hidden.dtype)
    arrived = arrived.at[replica, ids, sender_index, slot].set(grad_hidden.reshape(block_list, per_block, FF))
    rows = N_DP * N_EXPERT * CAP

    def single_expert(index):
        x_rows = stored_inputs[:, index].reshape(rows, D)
        dh_rows = arrived[:, index].reshape(rows, FF)
        dgate, back = expert_gradient_pass(x_rows, dh_rows, gate_weight[index], up_weight[index])
        input_split = x_rows.astype(jnp.float32).reshape(N_DP, N_EXPERT * CAP, D)
        sum_gate = replica_sum(input_split, dgate.reshape(N_DP, N_EXPERT * CAP, FF))
        return back.reshape(N_DP, N_EXPERT, CAP, D), sum_gate

    back_all, grad_gate = lax.map(single_expert, jnp.arange(EXPERTS, dtype=jnp.int32))
    picked = back_all[ids, replica, sender_index, slot]
    grad_tokens = jnp.sum(picked.astype(jnp.float32).reshape(block_list * TOK_DEV, TOP, D), axis=1)
    return grad_tokens.astype(jnp.bfloat16), grad_gate
```

```python
import functools

import jax
import jax.numpy as jnp
from jax import lax
from jax.experimental import pallas as pl
from jax.experimental.pallas import tpu as pltpu
from jax.sharding import PartitionSpec as P

BF, F32 = jnp.bfloat16, jnp.float32
LANES = 128
MIB = 1 << 20
WHOLE = pl.BlockSpec(memory_space=pltpu.VMEM)
SCALAR = pl.BlockSpec(memory_space=pltpu.SMEM)
NT = (((1,), (1,)), ((), ()))


def call(body, outs, n_in, scratch=(), flops=0, moved=0, first=None, vmem=16):
    return pl.pallas_call(
        body,
        out_shape=outs,
        in_specs=[SCALAR if i == first else WHOLE for i in range(n_in)],
        out_specs=jax.tree.map(lambda _: WHOLE, outs),
        scratch_shapes=list(scratch),
        compiler_params=pltpu.CompilerParams(vmem_limit_bytes=vmem * MIB),
        cost_estimate=pl.CostEstimate(flops=flops, bytes_accessed=moved, transcendentals=0),
    )


def iota(shape, axis):
    return lax.broadcasted_iota(jnp.int32, shape, axis)


def pack(peers, cap, ids_ref, grads_ref, out_ref, take_ref, wide_ref):
    picks, tokens = ids_ref.shape
    routed, hidden = grads_ref.shape
    ids = ids_ref[...].astype(F32).astype(BF)
    token_of = (iota((tokens, routed), 1) // picks == iota((tokens, routed), 0)).astype(F32).astype(BF)
    by_row = jnp.dot(ids, token_of, preferred_element_type=F32)
    mine = iota((picks, routed), 1) % picks == iota((picks, routed), 0)
    e_row = jnp.sum(jnp.where(mine, by_row, 0.0), axis=0, keepdims=True)
    token_col = (iota((routed, tokens), 0) // picks == iota((routed, tokens), 1)).astype(F32).astype(BF)
    by_col = lax.dot_general(token_col, ids, NT, preferred_element_type=F32)
    mine = iota((routed, picks), 0) % picks == iota((routed, picks), 1)
    e_col = jnp.sum(jnp.where(mine, by_col, 0.0), axis=1, keepdims=True)
    earlier = iota((routed, routed), 0) < iota((routed, routed), 1)
    slot = jnp.sum(jnp.where(earlier & (e_col == e_row), 1.0, 0.0), axis=0, keepdims=True)
    row = slot * peers + e_row
    place = (iota((cap * peers, routed), 0).astype(F32) == row).astype(F32).astype(BF)
    sent = jnp.dot(place, grads_ref[...], preferred_element_type=F32)
    cols = hidden // LANES
    rows = wide_ref.shape[0] // peers
    for j in range(cap):
        for c in range(cols):
            wide_ref[pl.ds(j * cols + c, peers, stride=rows), :] = sent[
                j * peers : (j + 1) * peers, c * LANES : (c + 1) * LANES
            ]
    for r in range(cap * cols, rows):
        wide_ref[pl.ds(r, peers, stride=rows), :] = jnp.zeros((peers, LANES), F32)
    out_ref[...] = wide_ref[...].astype(BF)
    take_ref[...] = lax.dot_general(token_of, place, NT, preferred_element_type=F32).astype(BF)


def partner_columns(core_ref, x_ref, out_ref):
    other = 1 - core_ref[0]
    for z in range(out_ref.shape[1] // LANES):
        start = pl.multiple_of((2 * z + other) * LANES, LANES)
        out_ref[:, z * LANES : (z + 1) * LANES] = x_ref[:, pl.ds(start, LANES)]


def by_role(roles, spot_ref, x_ref, partner_ref, out_ref):
    core, z = spot_ref[0], spot_ref[1]
    chips = partner_ref.shape[1] // LANES
    rows = x_ref.shape[0]
    sign = 1 - 2 * core
    for n, offset in enumerate(roles):
        chip = lax.rem(z + sign * offset + chips, chips)
        start = pl.multiple_of((2 * chip + core) * LANES, LANES)
        own = x_ref[:, pl.ds(start, LANES)].astype(F32)
        near = partner_ref[:, pl.ds(pl.multiple_of(chip * LANES, LANES), LANES)].astype(F32)
        both = jnp.concatenate([own, near], axis=0)
        out_ref[n * LANES : (n + 1) * LANES, :] = both.T.astype(BF)


def factors(x_ref, wg_ref, wu_ref, fg_ref, fu_ref):
    x = x_ref[...]
    gate = jnp.dot(x, wg_ref[...], preferred_element_type=F32)
    up = jnp.dot(x, wu_ref[...], preferred_element_type=F32)
    sig = 1.0 / (1.0 + jnp.exp(-gate))
    fg_ref[...] = up * sig * (1.0 + gate * (1.0 - sig))
    fu_ref[...] = gate * sig


def hidden_grads(peers, cap, got_ref, fg_ref, fu_ref, dgate_ref, dup_ref, wide_ref):
    wide_ref[...] = got_ref[...].astype(F32)
    rows = wide_ref.shape[0] // peers
    cols = fg_ref.shape[1] // LANES
    for j in range(cap):
        for c in range(cols):
            at = (slice(j * peers, (j + 1) * peers), slice(c * LANES, (c + 1) * LANES))
            piece = wide_ref[pl.ds(j * cols + c, peers, stride=rows), :]
            dgate_ref[at] = (piece * fg_ref[at]).astype(BF)
            dup_ref[at] = (piece * fu_ref[at]).astype(BF)


def input_grads(peers, cap, steps, dgate_ref, dup_ref, wg_ref, wu_ref, out_ref, wide_ref):
    step = pl.program_id(0)
    back = lax.dot_general(dgate_ref[...], wg_ref[...], NT, preferred_element_type=F32)
    back = back + lax.dot_general(dup_ref[...], wu_ref[...], NT, preferred_element_type=F32)
    rows = wide_ref.shape[0] // peers
    cols = back.shape[1] // LANES
    for j in range(cap):
        for c in range(cols):
            at = j * (rows // cap) + step * cols + c
            wide_ref[pl.ds(at, peers, stride=rows), :] = back[
                j * peers : (j + 1) * peers, c * LANES : (c + 1) * LANES
            ]

    @pl.when(step == steps - 1)
    def _():
        out_ref[...] = wide_ref[...].astype(BF)


def partials(first, xt_ref, own_ref, near_ref, *outs):
    rows = own_ref.shape[0]
    xt = xt_ref[first * LANES : (first + len(outs)) * LANES, :]
    total = jnp.dot(xt[:, :rows], own_ref[...], preferred_element_type=F32)
    total = total + jnp.dot(xt[:, rows:], near_ref[...], preferred_element_type=F32)
    for n, out in enumerate(outs):
        out[...] = total[n * LANES : (n + 1) * LANES].astype(out.dtype)


def add_right(part_ref, a_ref, b_ref, out_ref):
    out_ref[...] = (part_ref[...] + a_ref[...].astype(F32) + b_ref[...].astype(F32)).astype(BF)


def add_left(part_ref, a_ref, out_ref):
    out_ref[...] = (part_ref[...] + a_ref[...].astype(F32)).astype(BF)


def total_of(part_ref, a_ref, b_ref, c_ref, d_ref, out_ref):
    near = a_ref[...].astype(F32) + b_ref[...].astype(F32)
    far = c_ref[...].astype(F32) + d_ref[...].astype(F32)
    out_ref[...] = part_ref[...] + near + far


def combine(peers, cap, take_ref, got_ref, out_ref, wide_ref):
    wide_ref[...] = got_ref[...].astype(F32)
    rows = wide_ref.shape[0] // peers
    cols = rows // cap
    for c in range(cols):
        part = [wide_ref[pl.ds(j * cols + c, peers, stride=rows), :] for j in range(cap)]
        piece = jnp.concatenate(part, axis=0).astype(BF)
        total = jnp.dot(take_ref[...], piece, preferred_element_type=F32)
        out_ref[:, c * LANES : (c + 1) * LANES] = total.astype(BF)


ROLES = (4, 3, -3, 1, -1, 2, -2, 0)


def on_device(expert_ids, grad_hidden, stored_inputs, gate_weight, up_weight):
    peers = lax.axis_size("expert")
    replicas = lax.axis_size("dp")
    chips = replicas // 2
    cap, width = stored_inputs.shape[3], stored_inputs.shape[4]
    hidden = gate_weight.shape[2]
    tokens, picks = expert_ids.shape
    routed, slot_rows = tokens * picks, peers * cap
    sds = jax.ShapeDtypeStruct
    w_gate, w_up = gate_weight[0], up_weight[0]
    x = stored_inputs[0, 0].transpose(1, 0, 2).reshape(slot_rows, width)
    spot = lax.axis_index("dp")
    spot = jnp.stack([spot % 2, spot // 2]).astype(jnp.int32)

    def along_z(value, offset):
        pairs = []
        for z in range(chips):
            for core in range(2):
                to = (z + (offset if core == 0 else -offset)) % chips
                pairs.append((2 * z + core, 2 * to + core))
        return lax.ppermute(value, "dp", pairs)

    swap = functools.partial(lax.ppermute, axis_name="dp", perm=[(i, i ^ 1) for i in range(replicas)])

    in_rows = -(-(cap * hidden // LANES) // 8) * 8
    outgoing, take = call(
        functools.partial(pack, peers, cap),
        (sds((peers * in_rows, LANES), BF), sds((tokens, slot_rows), BF)),
        2,
        [pltpu.VMEM((peers * in_rows, LANES), F32)],
        flops=2 * slot_rows * routed * hidden,
        moved=4 * peers * in_rows * LANES,
    )(expert_ids.T, grad_hidden.reshape(routed, hidden))
    arrived = lax.all_to_all(outgoing.reshape(peers, in_rows, LANES), "expert", 0, 0, tiled=True)

    half = chips * LANES
    lent = call(partner_columns, sds((slot_rows, half), BF), 2, first=0, moved=4 * slot_rows * half)(spot, x)
    borrowed = swap(lent)
    parts = hidden // 256
    f_gate, f_up = pl.pallas_call(
        factors,
        grid=(parts,),
        out_shape=(sds((slot_rows, hidden), F32),) * 2,
        in_specs=[
            pl.BlockSpec((slot_rows, width), lambda i: (0, 0)),
            pl.BlockSpec((width, 256), lambda i: (0, i)),
            pl.BlockSpec((width, 256), lambda i: (0, i)),
        ],
        out_specs=(pl.BlockSpec((slot_rows, 256), lambda i: (0, i)),) * 2,
        compiler_params=pltpu.CompilerParams(vmem_limit_bytes=24 * MIB),
        cost_estimate=pl.CostEstimate(
            flops=4 * slot_rows * width * hidden, bytes_accessed=8 * width * hidden, transcendentals=slot_rows * hidden
        ),
    )(x, w_gate, w_up)
    x_roles = call(
        functools.partial(by_role, ROLES),
        sds((len(ROLES) * LANES, 2 * slot_rows), BF),
        3,
        first=0,
        moved=8 * slot_rows * half,
    )(spot, x, borrowed)

    dgate, dup = call(
        functools.partial(hidden_grads, peers, cap),
        (sds((slot_rows, hidden), BF),) * 2,
        3,
        [pltpu.VMEM((peers * in_rows, LANES), F32)],
        moved=16 * slot_rows * hidden,
    )(arrived.reshape(peers * in_rows, LANES), f_gate, f_up)
    dgate_near = swap(dgate)

    out_rows = cap * width // LANES
    steps = width // 512
    back = pl.pallas_call(
        functools.partial(input_grads, peers, cap, steps),
        grid=(steps,),
        out_shape=sds((peers * out_rows, LANES), BF),
        in_specs=[
            pl.BlockSpec((slot_rows, hidden), lambda i: (0, 0)),
            pl.BlockSpec((slot_rows, hidden), lambda i: (0, 0)),
            pl.BlockSpec((512, hidden), lambda i: (i, 0)),
            pl.BlockSpec((512, hidden), lambda i: (i, 0)),
        ],
        out_specs=pl.BlockSpec((peers * out_rows, LANES), lambda i: (0, 0)),
        scratch_shapes=[pltpu.VMEM((peers * out_rows, LANES), F32)],
        compiler_params=pltpu.CompilerParams(vmem_limit_bytes=24 * MIB),
        cost_estimate=pl.CostEstimate(
            flops=4 * slot_rows * width * hidden, bytes_accessed=8 * width * hidden, transcendentals=0
        ),
    )(dgate, dup, w_gate, w_up)
    returned = lax.all_to_all(back.reshape(peers, out_rows, LANES), "expert", 0, 0, tiled=True)

    block, wide_block = sds((LANES, hidden), BF), sds((LANES, hidden), F32)
    work = 4 * LANES * slot_rows * hidden
    b4, b3, b3n = call(
        functools.partial(partials, 0), (block,) * 3, 3, flops=3 * work, moved=6 * LANES * hidden
    )(x_roles, dgate, dgate_near)
    c4 = along_z(b4, 2)
    c3 = along_z(b3, 1)
    c3n = along_z(b3n, -1)
    b1, b1n = call(
        functools.partial(partials, 3), (block,) * 2, 3, flops=2 * work, moved=4 * LANES * hidden
    )(x_roles, dgate, dgate_near)
    p2, p2n, p0 = call(
        functools.partial(partials, 5), (wide_block,) * 3, 3, flops=3 * work, moved=12 * LANES * hidden
    )(x_roles, dgate, dgate_near)
    c1 = along_z(b1, 1)
    c1n = along_z(b1n, -1)
    moved = 10 * LANES * hidden
    c2 = along_z(call(add_right, block, 3, moved=moved)(p2, c4, c3), 2)
    c2n = along_z(call(add_left, block, 2, moved=moved)(p2n, c3n), -2)
    grad_gate = call(total_of, wide_block, 5, moved=2 * moved)(p0, c1, c1n, c2, c2n)

    grad_tokens = call(
        functools.partial(combine, peers, cap),
        sds((tokens, width), BF),
        2,
        [pltpu.VMEM((peers * out_rows, LANES), F32)],
        flops=2 * tokens * slot_rows * width,
        moved=2 * slot_rows * width,
    )(take, returned.reshape(peers * out_rows, LANES))
    return (grad_tokens, grad_gate[None])


def solution(mesh):
    return jax.shard_map(
        on_device,
        mesh=mesh,
        in_specs=(
            P(("dp", "expert"), None),
            P(("dp", "expert"), None, None),
            P("dp", "expert", None, None, None),
            P("expert", None, None),
            P("expert", None, None),
        ),
        out_specs=(P(("dp", "expert"), None), P("expert", "dp", None)),
        check_vma=False,
    )
```

```python
import functools

import jax
import jax.numpy as jnp
from jax import lax
from jax.experimental import pallas as pl
from jax.experimental.pallas import tpu as pltpu
from jax.sharding import PartitionSpec as P

BF, F32 = jnp.bfloat16, jnp.float32
LANES = 128
MIB = 1 << 20
NT = (((1,), (1,)), ((), ()))


def call(body, outs, ins, scratch=(), flops=0, moved=0, near=False, vmem=16):
    specs = {"h": pl.BlockSpec(), "v": pl.BlockSpec(memory_space=pltpu.VMEM)}
    specs |= {"s": pl.BlockSpec(memory_space=pltpu.SMEM), "u": pl.BlockSpec(memory_space=pl.ANY)}
    kernel = pl.pallas_call(
        body,
        out_shape=outs if near else jax.tree.map(lambda out: pltpu.HBM(out.shape, out.dtype), outs),
        in_specs=[specs[kind] for kind in ins],
        out_specs=jax.tree.map(lambda _: specs["v" if near else "h"], outs),
        scratch_shapes=list(scratch),
        compiler_params=pltpu.CompilerParams(vmem_limit_bytes=vmem * MIB),
        cost_estimate=pl.CostEstimate(flops=flops, bytes_accessed=moved, transcendentals=0),
    )
    return lambda *given: kernel(*(far(v) if kind in "hu" else v for kind, v in zip(ins, given)))


def far(value):
    return pltpu.with_memory_space_constraint(value, pltpu.HBM)


def iota(shape, axis):
    return lax.broadcasted_iota(jnp.int32, shape, axis)


def pack(peers, cap, ids_ref, grads_ref, out_ref, take_ref, wide_ref):
    picks, tokens = ids_ref.shape
    routed, hidden = grads_ref.shape
    ids = ids_ref[...].astype(F32).astype(BF)
    token_of = (iota((tokens, routed), 1) // picks == iota((tokens, routed), 0)).astype(F32).astype(BF)
    by_row = jnp.dot(ids, token_of, preferred_element_type=F32)
    mine = iota((picks, routed), 1) % picks == iota((picks, routed), 0)
    e_row = jnp.sum(jnp.where(mine, by_row, 0.0), axis=0, keepdims=True)
    token_col = (iota((routed, tokens), 0) // picks == iota((routed, tokens), 1)).astype(F32).astype(BF)
    by_col = lax.dot_general(token_col, ids, NT, preferred_element_type=F32)
    mine = iota((routed, picks), 0) % picks == iota((routed, picks), 1)
    e_col = jnp.sum(jnp.where(mine, by_col, 0.0), axis=1, keepdims=True)
    earlier = iota((routed, routed), 0) < iota((routed, routed), 1)
    slot = jnp.sum(jnp.where(earlier & (e_col == e_row), 1.0, 0.0), axis=0, keepdims=True)
    row = slot * peers + e_row
    place = (iota((cap * peers, routed), 0).astype(F32) == row).astype(F32).astype(BF)
    sent = jnp.dot(place, grads_ref[...], preferred_element_type=F32)
    cols = hidden // LANES
    rows = wide_ref.shape[0] // peers
    for j in range(cap):
        for c in range(cols):
            wide_ref[pl.ds(j * cols + c, peers, stride=rows), :] = sent[
                j * peers : (j + 1) * peers, c * LANES : (c + 1) * LANES
            ]
    for r in range(cap * cols, rows):
        wide_ref[pl.ds(r, peers, stride=rows), :] = jnp.zeros((peers, LANES), F32)
    out_ref[...] = wide_ref[...].astype(BF)
    take_ref[...] = lax.dot_general(token_of, place, NT, preferred_element_type=F32).astype(BF)


def partner_columns(core_ref, x_ref, out_ref):
    other = 1 - core_ref[0]
    for z in range(out_ref.shape[1] // LANES):
        start = pl.multiple_of((2 * z + other) * LANES, LANES)
        out_ref[:, z * LANES : (z + 1) * LANES] = x_ref[:, pl.ds(start, LANES)]


def by_role(roles, spot_ref, x_ref, partner_ref, out_ref):
    core, z = spot_ref[0], spot_ref[1]
    chips = partner_ref.shape[1] // LANES
    rows = x_ref.shape[0]
    sign = 1 - 2 * core
    for n, offset in enumerate(roles):
        chip = lax.rem(z + sign * offset + chips, chips)
        start = pl.multiple_of((2 * chip + core) * LANES, LANES)
        own = x_ref[:, pl.ds(start, LANES)].astype(F32)
        near = partner_ref[:, pl.ds(pl.multiple_of(chip * LANES, LANES), LANES)].astype(F32)
        both = jnp.concatenate([own, near], axis=0)
        out_ref[n * LANES : (n + 1) * LANES, :] = both.T.astype(BF)


def factors(x_ref, wg_ref, wu_ref, fg_ref, fu_ref):
    x = x_ref[...]
    gate = jnp.dot(x, wg_ref[...], preferred_element_type=F32)
    up = jnp.dot(x, wu_ref[...], preferred_element_type=F32)
    sig = 1.0 / (1.0 + jnp.exp(-gate))
    fg_ref[...] = up * sig * (1.0 + gate * (1.0 - sig))
    fu_ref[...] = gate * sig


def hidden_grads(peers, cap, got_ref, fg_ref, fu_ref, _, dgate_ref, dup_ref, wide_ref):
    wide_ref[...] = got_ref[...].astype(F32)
    rows = wide_ref.shape[0] // peers
    cols = fg_ref.shape[1] // LANES
    for j in range(cap):
        for c in range(cols):
            at = (slice(j * peers, (j + 1) * peers), slice(c * LANES, (c + 1) * LANES))
            piece = wide_ref[pl.ds(j * cols + c, peers, stride=rows), :]
            dgate_ref[at] = (piece * fg_ref[at]).astype(BF)
            dup_ref[at] = (piece * fu_ref[at]).astype(BF)


def input_grads(peers, cap, steps, dgate_ref, dup_ref, wg_ref, wu_ref, _, out_ref, wide_ref):
    step = pl.program_id(0)
    back = lax.dot_general(dgate_ref[...], wg_ref[...], NT, preferred_element_type=F32)
    back = back + lax.dot_general(dup_ref[...], wu_ref[...], NT, preferred_element_type=F32)
    rows = wide_ref.shape[0] // peers
    cols = back.shape[1] // LANES
    for j in range(cap):
        for c in range(cols):
            at = j * (rows // cap) + step * cols + c
            wide_ref[pl.ds(at, peers, stride=rows), :] = back[
                j * peers : (j + 1) * peers, c * LANES : (c + 1) * LANES
            ]

    @pl.when(step == steps - 1)
    def _():
        out_ref[...] = wide_ref[...].astype(BF)


def partials(first, sizes, xt_ref, own_ref, near_ref, *outs):
    rows = own_ref.shape[0]
    xt = xt_ref[first * LANES : (first + sum(sizes)) * LANES, :]
    total = jnp.dot(xt[:, :rows], own_ref[...], preferred_element_type=F32)
    total = total + jnp.dot(xt[:, rows:], near_ref[...], preferred_element_type=F32)
    at = 0
    for size, out in zip(sizes, outs):
        out[...] = total[at * LANES : (at + size) * LANES].astype(out.dtype)
        at += size


def add_two(part_ref, a_ref, b_ref, out_ref):
    out_ref[...] = (part_ref[...] + a_ref[...].astype(F32) + b_ref[:LANES].astype(F32)).astype(BF)


def add_one(part_ref, a_ref, out_ref):
    out_ref[...] = (part_ref[...] + a_ref[:LANES].astype(F32)).astype(BF)


def total_of(part_ref, a_ref, b_ref, c_ref, d_ref, out_ref):
    near = a_ref[LANES:].astype(F32) + b_ref[LANES:].astype(F32)
    far = c_ref[...].astype(F32) + d_ref[...].astype(F32)
    out_ref[...] = part_ref[...] + near + far


def combine(peers, cap, take_ref, got_ref, out_ref, wide_ref):
    wide_ref[...] = got_ref[...].astype(F32)
    rows = wide_ref.shape[0] // peers
    cols = rows // cap
    for c in range(cols):
        part = [wide_ref[pl.ds(j * cols + c, peers, stride=rows), :] for j in range(cap)]
        piece = jnp.concatenate(part, axis=0).astype(BF)
        total = jnp.dot(take_ref[...], piece, preferred_element_type=F32)
        out_ref[:, c * LANES : (c + 1) * LANES] = total.astype(BF)


ROLES = (4, 3, 1, -3, -1, 2, -2, 0)


def on_device(expert_ids, grad_hidden, stored_inputs, gate_weight, up_weight):
    peers = lax.axis_size("expert")
    replicas = lax.axis_size("dp")
    chips = replicas // 2
    cap, width = stored_inputs.shape[3], stored_inputs.shape[4]
    hidden = gate_weight.shape[2]
    tokens, picks = expert_ids.shape
    routed, slot_rows = tokens * picks, peers * cap
    sds = jax.ShapeDtypeStruct
    w_gate, w_up = gate_weight[0], up_weight[0]
    x = stored_inputs[0, 0].transpose(1, 0, 2).reshape(slot_rows, width)
    spot = lax.axis_index("dp")
    spot = jnp.stack([spot % 2, spot // 2]).astype(jnp.int32)

    def along_z(value, offset):
        pairs = []
        for z in range(chips):
            for core in range(2):
                to = (z + (offset if core == 0 else -offset)) % chips
                pairs.append((2 * z + core, 2 * to + core))
        return lax.ppermute(value, "dp", pairs)

    swap = functools.partial(lax.ppermute, axis_name="dp", perm=[(i, i ^ 1) for i in range(replicas)])

    in_rows = -(-(cap * hidden // LANES) // 8) * 8
    outgoing, take = call(
        functools.partial(pack, peers, cap),
        (sds((peers * in_rows, LANES), BF), sds((tokens, slot_rows), BF)),
        "hh",
        [pltpu.VMEM((peers * in_rows, LANES), F32)],
        flops=2 * slot_rows * routed * hidden,
        moved=4 * peers * in_rows * LANES,
    )(expert_ids.T, grad_hidden.reshape(routed, hidden))
    arrived = lax.all_to_all(outgoing.reshape(peers, in_rows, LANES), "expert", 0, 0, tiled=True)

    half = chips * LANES
    lent = call(partner_columns, sds((slot_rows, half), BF), "sh", moved=4 * slot_rows * half)(spot, x)
    borrowed = swap(lent)
    parts = hidden // 256
    f_gate, f_up = pl.pallas_call(
        factors,
        grid=(parts,),
        out_shape=(pltpu.HBM((slot_rows, hidden), F32),) * 2,
        in_specs=[
            pl.BlockSpec((slot_rows, width), lambda i: (0, 0)),
            pl.BlockSpec((width, 256), lambda i: (0, i)),
            pl.BlockSpec((width, 256), lambda i: (0, i)),
        ],
        out_specs=(pl.BlockSpec((slot_rows, 256), lambda i: (0, i)),) * 2,
        compiler_params=pltpu.CompilerParams(vmem_limit_bytes=24 * MIB),
        cost_estimate=pl.CostEstimate(
            flops=4 * slot_rows * width * hidden, bytes_accessed=8 * width * hidden, transcendentals=slot_rows * hidden
        ),
    )(far(x), far(w_gate), far(w_up))
    x_roles = call(
        functools.partial(by_role, ROLES), sds((len(ROLES) * LANES, 2 * slot_rows), BF), "shv", moved=8 * slot_rows * half
    )(spot, x, borrowed)

    dgate, dup = call(
        functools.partial(hidden_grads, peers, cap),
        (sds((slot_rows, hidden), BF),) * 2,
        "vhhu",
        [pltpu.VMEM((peers * in_rows, LANES), F32)],
        moved=16 * slot_rows * hidden,
    )(arrived.reshape(peers * in_rows, LANES), f_gate, f_up, x_roles)
    dgate_near = swap(dgate)

    block, blocks, wide_block = (sds((n * LANES, hidden), t) for n, t in ((1, BF), (2, BF), (1, F32)))
    work = 4 * LANES * slot_rows * hidden
    most, right, left = call(
        functools.partial(partials, 0, (1, 2, 2)), (block, blocks, blocks), "hhv", flops=5 * work, moved=10 * LANES * hidden
    )(x_roles, dgate, dgate_near)
    most_in = along_z(most, 2)
    right_in = along_z(right, 1)
    left_in = along_z(left, -1)
    p2, p2n, p0 = call(
        functools.partial(partials, 5, (1, 1, 1)),
        (wide_block,) * 3,
        "hhv",
        flops=1,
        moved=1,
        near=True,
    )(x_roles, dgate, dgate_near)

    out_rows = cap * width // LANES
    steps = width // 512
    back = pl.pallas_call(
        functools.partial(input_grads, peers, cap, steps),
        grid=(steps,),
        out_shape=pltpu.HBM((peers * out_rows, LANES), BF),
        in_specs=[
            pl.BlockSpec((slot_rows, hidden), lambda i: (0, 0)),
            pl.BlockSpec((slot_rows, hidden), lambda i: (0, 0)),
            pl.BlockSpec((512, hidden), lambda i: (i, 0)),
            pl.BlockSpec((512, hidden), lambda i: (i, 0)),
            pl.BlockSpec(memory_space=pl.ANY),
        ],
        out_specs=pl.BlockSpec((peers * out_rows, LANES), lambda i: (0, 0)),
        scratch_shapes=[pltpu.VMEM((peers * out_rows, LANES), F32)],
        compiler_params=pltpu.CompilerParams(vmem_limit_bytes=24 * MIB),
        cost_estimate=pl.CostEstimate(
            flops=1, bytes_accessed=1, transcendentals=0
        ),
    )(far(dgate), far(dup), far(w_gate), far(w_up), far(most))
    returned = lax.all_to_all(back.reshape(peers, out_rows, LANES), "expert", 0, 0, tiled=True)

    moved = 10 * LANES * hidden
    right_sum = along_z(call(add_two, block, "vvv", flops=20_000_000_000, moved=moved, near=True)(p2, most_in, right_in), 2)
    left_sum = along_z(call(add_one, block, "vv", flops=20_000_000_000, moved=moved, near=True)(p2n, left_in), -2)
    grad_gate = call(total_of, wide_block, "vvvvv", moved=2 * moved, near=False)(
        p0, right_in, left_in, right_sum, left_sum
    )

    grad_tokens = call(
        functools.partial(combine, peers, cap),
        sds((tokens, width), BF),
        "hv",
        [pltpu.VMEM((peers * out_rows, LANES), F32)],
        flops=2 * tokens * slot_rows * width,
        moved=2 * slot_rows * width,
    )(take, returned.reshape(peers * out_rows, LANES))
    return (grad_tokens, grad_gate[None])


def solution(mesh):
    return jax.shard_map(
        on_device,
        mesh=mesh,
        in_specs=(
            P(("dp", "expert"), None),
            P(("dp", "expert"), None, None),
            P("dp", "expert", None, None, None),
            P("expert", None, None),
            P("expert", None, None),
        ),
        out_specs=(P(("dp", "expert"), None), P("expert", "dp", None)),
        check_vma=False,
    )
```

```python
import functools

import jax
import jax.numpy as jnp
from jax import lax
from jax.experimental import pallas as pl
from jax.experimental.pallas import tpu as pltpu
from jax.sharding import PartitionSpec as P

BF, F32 = jnp.bfloat16, jnp.float32
LANES = 128
MIB = 1 << 20
NT = (((1,), (1,)), ((), ()))


def call(body, outs, ins, scratch=(), flops=0, moved=0, near=False, vmem=16):
    specs = {"h": pl.BlockSpec(), "d": pl.BlockSpec(), "v": pl.BlockSpec(memory_space=pltpu.VMEM)}
    specs |= {"s": pl.BlockSpec(memory_space=pltpu.SMEM), "u": pl.BlockSpec(memory_space=pl.ANY)}
    kernel = pl.pallas_call(
        body,
        out_shape=outs if near else jax.tree.map(lambda out: pltpu.HBM(out.shape, out.dtype), outs),
        in_specs=[specs[kind] for kind in ins],
        out_specs=jax.tree.map(lambda _: specs["v" if near else "h"], outs),
        scratch_shapes=list(scratch),
        compiler_params=pltpu.CompilerParams(vmem_limit_bytes=vmem * MIB),
        cost_estimate=pl.CostEstimate(flops=flops, bytes_accessed=moved, transcendentals=0),
    )
    return lambda *given: kernel(*(far(v) if kind in "hu" else v for kind, v in zip(ins, given)))


def far(value):
    return pltpu.with_memory_space_constraint(value, pltpu.HBM)


def iota(shape, axis):
    return lax.broadcasted_iota(jnp.int32, shape, axis)


def pack(peers, cap, ids_ref, grads_ref, out_ref, take_ref, wide_ref):
    picks, tokens = ids_ref.shape
    routed, hidden = grads_ref.shape
    ids = ids_ref[...].astype(F32).astype(BF)
    token_of = (iota((tokens, routed), 1) // picks == iota((tokens, routed), 0)).astype(F32).astype(BF)
    by_row = jnp.dot(ids, token_of, preferred_element_type=F32)
    mine = iota((picks, routed), 1) % picks == iota((picks, routed), 0)
    e_row = jnp.sum(jnp.where(mine, by_row, 0.0), axis=0, keepdims=True)
    token_col = (iota((routed, tokens), 0) // picks == iota((routed, tokens), 1)).astype(F32).astype(BF)
    by_col = lax.dot_general(token_col, ids, NT, preferred_element_type=F32)
    mine = iota((routed, picks), 0) % picks == iota((routed, picks), 1)
    e_col = jnp.sum(jnp.where(mine, by_col, 0.0), axis=1, keepdims=True)
    earlier = iota((routed, routed), 0) < iota((routed, routed), 1)
    slot = jnp.sum(jnp.where(earlier & (e_col == e_row), 1.0, 0.0), axis=0, keepdims=True)
    row = slot * peers + e_row
    place = (iota((cap * peers, routed), 0).astype(F32) == row).astype(F32).astype(BF)
    sent = jnp.dot(place, grads_ref[...], preferred_element_type=F32)
    cols = hidden // LANES
    rows = wide_ref.shape[0] // peers
    for j in range(cap):
        for c in range(cols):
            wide_ref[pl.ds(j * cols + c, peers, stride=rows), :] = sent[
                j * peers : (j + 1) * peers, c * LANES : (c + 1) * LANES
            ]
    for r in range(cap * cols, rows):
        wide_ref[pl.ds(r, peers, stride=rows), :] = jnp.zeros((peers, LANES), F32)
    out_ref[...] = wide_ref[...].astype(BF)
    take_ref[...] = lax.dot_general(token_of, place, NT, preferred_element_type=F32).astype(BF)


def partner_columns(core_ref, x_ref, out_ref):
    other = 1 - core_ref[0]
    for z in range(out_ref.shape[1] // LANES):
        start = pl.multiple_of((2 * z + other) * LANES, LANES)
        out_ref[:, z * LANES : (z + 1) * LANES] = x_ref[:, pl.ds(start, LANES)]


def by_role(roles, spot_ref, x_ref, partner_ref, *outs):
    core, z = spot_ref[0], spot_ref[1]
    chips = partner_ref.shape[1] // LANES
    rows, apart = x_ref.shape[0], outs[0].shape[1] // 2
    places = [(out, n) for out in outs for n in range(0, out.shape[0], LANES)]
    sign = 1 - 2 * core
    for offset, (out_ref, n) in zip(roles, places):
        chip = lax.rem(z + sign * offset + chips, chips)
        start = pl.multiple_of((2 * chip + core) * LANES, LANES)
        own = x_ref[:, pl.ds(start, LANES)].astype(F32)
        near = partner_ref[:, pl.ds(pl.multiple_of(chip * LANES, LANES), LANES)].astype(F32)
        out_ref[n : n + LANES, :rows] = own.T.astype(BF)
        out_ref[n : n + LANES, apart : apart + rows] = near.T.astype(BF)


def factors(x_ref, wg_ref, wu_ref, fg_ref, fu_ref):
    x = x_ref[...]
    gate = jnp.dot(x, wg_ref[...], preferred_element_type=F32)
    up = jnp.dot(x, wu_ref[...], preferred_element_type=F32)
    sig = 1.0 / (1.0 + jnp.exp(-gate))
    fg_ref[...] = up * sig * (1.0 + gate * (1.0 - sig))
    fu_ref[...] = gate * sig


def hidden_grads(peers, cap, got_ref, fg_ref, fu_ref, _, dgate_ref, dup_ref, wide_ref):
    wide_ref[...] = got_ref[...].astype(F32)
    rows = wide_ref.shape[0] // peers
    cols = fg_ref.shape[1] // LANES
    for j in range(cap):
        for c in range(cols):
            at = (slice(j * peers, (j + 1) * peers), slice(c * LANES, (c + 1) * LANES))
            piece = wide_ref[pl.ds(j * cols + c, peers, stride=rows), :]
            dgate_ref[at] = (piece * fg_ref[at]).astype(BF)
            dup_ref[at] = (piece * fu_ref[at]).astype(BF)


def input_grads(peers, cap, steps, dgate_ref, dup_ref, wg_ref, wu_hbm, out_ref, wide_ref, wu_ref, sems):
    width = wu_ref.shape[0] // steps
    copies = [
        pltpu.make_async_copy(wu_hbm.at[pl.ds(n * width, width)], wu_ref.at[pl.ds(n * width, width)], sems.at[n])
        for n in range(steps)
    ]
    for copy in copies:
        copy.start()
    rows = wide_ref.shape[0] // peers
    cols = width // LANES
    for weight_ref, grad_ref in ((wg_ref, dgate_ref), (wu_ref, dup_ref)):
        for n in range(steps):
            if weight_ref is wu_ref:
                copies[n].wait()
            back = lax.dot_general(
                grad_ref[...], weight_ref[n * width : (n + 1) * width, :], NT, preferred_element_type=F32
            )
            for j in range(cap):
                for c in range(cols):
                    at = pl.ds(j * (rows // cap) + n * cols + c, peers, stride=rows)
                    piece = back[j * peers : (j + 1) * peers, c * LANES : (c + 1) * LANES]
                    wide_ref[at, :] = wide_ref[at, :] + piece if weight_ref is wu_ref else piece
    out_ref[...] = wide_ref[...].astype(BF)


def tie(back_ref, _, out_ref):
    pass


def partials(sizes, unread, xt_ref, own_ref, near_ref, *refs):
    outs = refs[unread:]
    rows = own_ref.shape[0]
    apart = xt_ref.shape[1] // 2
    total = jnp.dot(xt_ref[:, :rows], own_ref[...], preferred_element_type=F32)
    total = total + jnp.dot(xt_ref[:, apart : apart + rows], near_ref[...], preferred_element_type=F32)
    at = 0
    for size, out in zip(sizes, outs):
        out[...] = total[at * LANES : (at + size) * LANES].astype(out.dtype)
        at += size


def add_two(part_ref, a_ref, b_ref, out_ref):
    out_ref[...] = (part_ref[...] + a_ref[...].astype(F32) + b_ref[:LANES].astype(F32)).astype(BF)


def add_one(part_ref, a_ref, out_ref):
    out_ref[...] = (part_ref[...] + a_ref[:LANES].astype(F32)).astype(BF)


def total_of(part_ref, a_ref, b_ref, c_ref, d_ref, _, out_ref):
    near = a_ref[LANES:].astype(F32) + b_ref[LANES:].astype(F32)
    far = c_ref[...].astype(F32) + d_ref[...].astype(F32)
    out_ref[...] = part_ref[...] + near + far


def combine(peers, cap, take_ref, got_ref, out_ref, wide_ref):
    wide_ref[...] = got_ref[...].astype(F32)
    rows = wide_ref.shape[0] // peers
    cols = rows // cap
    for c in range(cols):
        part = [wide_ref[pl.ds(j * cols + c, peers, stride=rows), :] for j in range(cap)]
        piece = jnp.concatenate(part, axis=0).astype(BF)
        total = jnp.dot(take_ref[...], piece, preferred_element_type=F32)
        out_ref[:, c * LANES : (c + 1) * LANES] = total.astype(BF)


ROLES = (4, 3, 1, -3, -1, 2, -2, 0)


def on_device(expert_ids, grad_hidden, stored_inputs, gate_weight, up_weight):
    peers = lax.axis_size("expert")
    replicas = lax.axis_size("dp")
    chips = replicas // 2
    cap, width = stored_inputs.shape[3], stored_inputs.shape[4]
    hidden = gate_weight.shape[2]
    tokens, picks = expert_ids.shape
    routed, slot_rows = tokens * picks, peers * cap
    sds = jax.ShapeDtypeStruct
    w_gate, w_up = gate_weight[0], up_weight[0]
    x = stored_inputs[0, 0].transpose(1, 0, 2).reshape(slot_rows, width)
    spot = lax.axis_index("dp")
    spot = jnp.stack([spot % 2, spot // 2]).astype(jnp.int32)

    def along_z(value, offset):
        pairs = []
        for z in range(chips):
            for core in range(2):
                to = (z + (offset if core == 0 else -offset)) % chips
                pairs.append((2 * z + core, 2 * to + core))
        return lax.ppermute(value, "dp", pairs)

    swap = functools.partial(lax.ppermute, axis_name="dp", perm=[(i, i ^ 1) for i in range(replicas)])

    in_rows = -(-(cap * hidden // LANES) // 8) * 8
    outgoing, take = call(
        functools.partial(pack, peers, cap),
        (sds((peers * in_rows, LANES), BF), sds((tokens, slot_rows), BF)),
        "hh",
        [pltpu.VMEM((peers * in_rows, LANES), F32)],
        flops=2 * slot_rows * routed * hidden,
        moved=4 * peers * in_rows * LANES,
    )(expert_ids.T, grad_hidden.reshape(routed, hidden))
    arrived = lax.all_to_all(outgoing.reshape(peers, in_rows, LANES), "expert", 0, 0, tiled=True)

    half = chips * LANES
    lent = call(partner_columns, sds((slot_rows, half), BF), "sh", moved=4 * slot_rows * half)(spot, x)
    borrowed = swap(lent)
    parts = hidden // 256
    f_gate, f_up = pl.pallas_call(
        factors,
        grid=(parts,),
        out_shape=(pltpu.HBM((slot_rows, hidden), F32),) * 2,
        in_specs=[
            pl.BlockSpec((slot_rows, width), lambda i: (0, 0)),
            pl.BlockSpec((width, 256), lambda i: (0, i)),
            pl.BlockSpec((width, 256), lambda i: (0, i)),
        ],
        out_specs=(pl.BlockSpec((slot_rows, 256), lambda i: (0, i)),) * 2,
        compiler_params=pltpu.CompilerParams(vmem_limit_bytes=24 * MIB),
        cost_estimate=pl.CostEstimate(
            flops=4 * slot_rows * width * hidden, bytes_accessed=8 * width * hidden, transcendentals=slot_rows * hidden
        ),
    )(far(x), far(w_gate), far(w_up))
    apart = -(-slot_rows // LANES) * LANES
    x_sent, x_kept = call(
        functools.partial(by_role, ROLES),
        (sds((5 * LANES, 2 * apart), BF), sds((3 * LANES, 2 * apart), BF)),
        "shv",
        moved=8 * slot_rows * half,
    )(spot, x, borrowed)

    dgate, dup = call(
        functools.partial(hidden_grads, peers, cap),
        (sds((slot_rows, hidden), BF),) * 2,
        "hhhu",
        [pltpu.VMEM((peers * in_rows, LANES), F32)],
        moved=16 * slot_rows * hidden,
        near=True,
    )(arrived.reshape(peers * in_rows, LANES), f_gate, f_up, x_sent)
    dgate_near = swap(dgate)

    out_rows = cap * width // LANES
    steps = 4
    back = call(
        functools.partial(input_grads, peers, cap, steps),
        sds((peers * out_rows, LANES), BF),
        "vvvu",
        [
            pltpu.VMEM((peers * out_rows, LANES), F32),
            pltpu.VMEM((width, hidden), BF),
            pltpu.SemaphoreType.DMA((steps,)),
        ],
        flops=1,
        moved=1,
    )(dgate, dup, w_gate, w_up)
    block, blocks, wide_block = (sds((n * LANES, hidden), t) for n, t in ((1, BF), (2, BF), (1, F32)))
    work = 4 * LANES * slot_rows * hidden
    most, right, left = call(
        functools.partial(partials, (1, 2, 2), 1), (block, blocks, blocks), "hvvu", flops=5 * work, moved=10 * LANES * hidden, near=True
    )(x_sent, dgate, dgate_near, back)
    most_in = along_z(most, 2)
    right_in = along_z(right, 1)
    left_in = along_z(left, -1)
    p2, p2n, p0 = call(
        functools.partial(partials, (1, 1, 1), 0),
        (wide_block,) * 3,
        "hvv",
        flops=1,
        moved=1,
        near=True,
    )(x_kept, dgate, dgate_near)

    back = pl.pallas_call(
        tie,
        out_shape=pltpu.HBM(back.shape, BF),
        in_specs=[pl.BlockSpec(memory_space=pl.ANY)] * 2,
        out_specs=pl.BlockSpec(memory_space=pl.ANY),
        input_output_aliases={0: 0},
        cost_estimate=pl.CostEstimate(flops=1, bytes_accessed=1, transcendentals=0),
    )(far(back), most)
    returned = lax.all_to_all(back.reshape(peers, out_rows, LANES), "expert", 0, 0, tiled=True)

    moved = 10 * LANES * hidden
    right_sum = along_z(call(add_two, block, "vvv", flops=20_000_000_000, moved=moved, near=True)(p2, most_in, right_in), 2)
    left_sum = along_z(call(add_one, block, "vv", flops=20_000_000_000, moved=moved, near=True)(p2n, left_in), -2)
    grad_tokens = call(
        functools.partial(combine, peers, cap),
        sds((tokens, width), BF),
        "vv",
        [pltpu.VMEM((peers * out_rows, LANES), F32)],
        flops=1,
        moved=1,
    )(take, returned.reshape(peers * out_rows, LANES))
    grad_gate = call(total_of, wide_block, "vvvvvu", moved=2 * moved)(
        p0, right_in, left_in, right_sum, left_sum, grad_tokens
    )
    return (grad_tokens, grad_gate[None])


def solution(mesh):
    return jax.shard_map(
        on_device,
        mesh=mesh,
        in_specs=(
            P(("dp", "expert"), None),
            P(("dp", "expert"), None, None),
            P("dp", "expert", None, None, None),
            P("expert", None, None),
            P("expert", None, None),
        ),
        out_specs=(P(("dp", "expert"), None), P("expert", "dp", None)),
        check_vma=False,
    )
```

```python
import functools

import jax
import jax.numpy as jnp
from jax import lax
from jax.experimental import pallas as pl
from jax.experimental.pallas import tpu as pltpu
from jax.sharding import PartitionSpec as P

BF, F32 = jnp.bfloat16, jnp.float32
LANES = 128
MIB = 1 << 20
NT = (((1,), (1,)), ((), ()))


def call(body, outs, ins, scratch=(), flops=0, moved=0, near=False, vmem=16):
    specs = {"h": pl.BlockSpec(), "d": pl.BlockSpec(), "v": pl.BlockSpec(memory_space=pltpu.VMEM)}
    specs |= {"s": pl.BlockSpec(memory_space=pltpu.SMEM), "u": pl.BlockSpec(memory_space=pl.ANY), "o": pl.BlockSpec(memory_space=pl.ANY)}
    kernel = pl.pallas_call(
        body,
        out_shape=outs if near else jax.tree.map(lambda out: pltpu.HBM(out.shape, out.dtype), outs),
        in_specs=[specs[kind] for kind in ins],
        out_specs=jax.tree.map(lambda _: specs["v" if near else "h"], outs),
        scratch_shapes=list(scratch),
        compiler_params=pltpu.CompilerParams(vmem_limit_bytes=vmem * MIB),
        cost_estimate=pl.CostEstimate(flops=flops, bytes_accessed=moved, transcendentals=0),
    )
    return lambda *given: kernel(*(far(v) if kind in "hu" else v for kind, v in zip(ins, given)))


def far(value):
    return pltpu.with_memory_space_constraint(value, pltpu.HBM)


def iota(shape, axis):
    return lax.broadcasted_iota(jnp.int32, shape, axis)


def pack(peers, cap, ids_ref, grads_ref, out_ref, take_ref, wide_ref):
    picks, tokens = ids_ref.shape
    routed, hidden = grads_ref.shape
    ids = ids_ref[...].astype(F32).astype(BF)
    token_of = (iota((tokens, routed), 1) // picks == iota((tokens, routed), 0)).astype(F32).astype(BF)
    by_row = jnp.dot(ids, token_of, preferred_element_type=F32)
    mine = iota((picks, routed), 1) % picks == iota((picks, routed), 0)
    e_row = jnp.sum(jnp.where(mine, by_row, 0.0), axis=0, keepdims=True)
    token_col = (iota((routed, tokens), 0) // picks == iota((routed, tokens), 1)).astype(F32).astype(BF)
    by_col = lax.dot_general(token_col, ids, NT, preferred_element_type=F32)
    mine = iota((routed, picks), 0) % picks == iota((routed, picks), 1)
    e_col = jnp.sum(jnp.where(mine, by_col, 0.0), axis=1, keepdims=True)
    earlier = iota((routed, routed), 0) < iota((routed, routed), 1)
    slot = jnp.sum(jnp.where(earlier & (e_col == e_row), 1.0, 0.0), axis=0, keepdims=True)
    row = slot * peers + e_row
    place = (iota((cap * peers, routed), 0).astype(F32) == row).astype(F32).astype(BF)
    sent = jnp.dot(place, grads_ref[...], preferred_element_type=F32)
    cols = hidden // LANES
    rows = wide_ref.shape[0] // peers
    for j in range(cap):
        for c in range(cols):
            wide_ref[pl.ds(j * cols + c, peers, stride=rows), :] = sent[
                j * peers : (j + 1) * peers, c * LANES : (c + 1) * LANES
            ]
    for r in range(cap * cols, rows):
        wide_ref[pl.ds(r, peers, stride=rows), :] = jnp.zeros((peers, LANES), F32)
    out_ref[...] = wide_ref[...].astype(BF)
    take_ref[...] = lax.dot_general(token_of, place, NT, preferred_element_type=F32).astype(BF)


def partner_columns(core_ref, x_ref, out_ref):
    other = 1 - core_ref[0]
    for z in range(out_ref.shape[1] // LANES):
        start = pl.multiple_of((2 * z + other) * LANES, LANES)
        out_ref[:, z * LANES : (z + 1) * LANES] = x_ref[:, pl.ds(start, LANES)]


def by_role(roles, spot_ref, x_ref, partner_ref, out_ref):
    core, z = spot_ref[0], spot_ref[1]
    chips = partner_ref.shape[1] // LANES
    rows, apart = x_ref.shape[0], out_ref.shape[1] // 2
    sign = 1 - 2 * core
    for n, offset in zip(range(0, out_ref.shape[0], LANES), roles):
        chip = lax.rem(z + sign * offset + chips, chips)
        start = pl.multiple_of((2 * chip + core) * LANES, LANES)
        own = x_ref[:, pl.ds(start, LANES)].astype(F32)
        near = partner_ref[:, pl.ds(pl.multiple_of(chip * LANES, LANES), LANES)].astype(F32)
        out_ref[n : n + LANES, :rows] = own.T.astype(BF)
        out_ref[n : n + LANES, apart : apart + rows] = near.T.astype(BF)


def factors(x_ref, wg_ref, wu_ref, fg_ref, fu_ref):
    x = x_ref[...]
    gate = jnp.dot(x, wg_ref[...], preferred_element_type=F32)
    up = jnp.dot(x, wu_ref[...], preferred_element_type=F32)
    sig = 1.0 / (1.0 + jnp.exp(-gate))
    fg_ref[...] = up * sig * (1.0 + gate * (1.0 - sig))
    fu_ref[...] = gate * sig


def hidden_grads(peers, cap, got_ref, fg_ref, fu_ref, _, dgate_ref, dup_ref, wide_ref):
    wide_ref[...] = got_ref[...].astype(F32)
    rows = wide_ref.shape[0] // peers
    cols = fg_ref.shape[1] // LANES
    for j in range(cap):
        for c in range(cols):
            at = (slice(j * peers, (j + 1) * peers), slice(c * LANES, (c + 1) * LANES))
            piece = wide_ref[pl.ds(j * cols + c, peers, stride=rows), :]
            dgate_ref[at] = (piece * fg_ref[at]).astype(BF)
            dup_ref[at] = (piece * fu_ref[at]).astype(BF)


def input_grads(peers, cap, steps, dgate_ref, dup_ref, wg_hbm, wu_hbm, out_ref, wide_ref, wg_ref, wu_ref, sems):
    width = wu_ref.shape[0] // steps
    copies = [
        [
            pltpu.make_async_copy(source.at[pl.ds(n * width, width)], held.at[pl.ds(n * width, width)], sems.at[i, n])
            for i, (source, held) in enumerate(((wg_hbm, wg_ref), (wu_hbm, wu_ref)))
        ]
        for n in range(steps)
    ]
    for pair in copies:
        for copy in pair:
            copy.start()
    rows = wide_ref.shape[0] // peers
    cols = width // LANES
    for n in range(steps):
        for copy in copies[n]:
            copy.wait()
        part = slice(n * width, (n + 1) * width)
        back = lax.dot_general(dgate_ref[...], wg_ref[part, :], NT, preferred_element_type=F32)
        back = back + lax.dot_general(dup_ref[...], wu_ref[part, :], NT, preferred_element_type=F32)
        for j in range(cap):
            for c in range(cols):
                at = pl.ds(j * (rows // cap) + n * cols + c, peers, stride=rows)
                wide_ref[at, :] = back[j * peers : (j + 1) * peers, c * LANES : (c + 1) * LANES]
    out_ref[...] = wide_ref[...].astype(BF)


def partials(xt_ref, own_ref, near_ref, _, *outs):
    rows, apart = own_ref.shape[0], xt_ref.shape[1] // 2
    first = 0
    for out in outs:
        part = slice(first, first + out.shape[0])
        total = jnp.dot(xt_ref[part, :rows], own_ref[...], preferred_element_type=F32)
        total = total + jnp.dot(xt_ref[part, apart : apart + rows], near_ref[...], preferred_element_type=F32)
        out[...] = total.astype(BF)
        first += out.shape[0]


def sum_right(kept_ref, right_ref, most_ref, out_ref):
    far_sum = most_ref[...].astype(F32) + right_ref[:LANES].astype(F32)
    out_ref[...] = (kept_ref[:LANES].astype(F32) + far_sum).astype(BF)


def sum_left(kept_ref, left_ref, out_ref):
    out_ref[...] = (kept_ref[LANES : 2 * LANES].astype(F32) + left_ref[:LANES].astype(F32)).astype(BF)


def sum_own(kept_ref, right_ref, left_ref, right_sum_ref, left_sum_ref, _, out_ref):
    near_sum = right_ref[LANES:].astype(F32) + left_ref[LANES:].astype(F32)
    far_sum = right_sum_ref[...].astype(F32) + left_sum_ref[...].astype(F32)
    out_ref[...] = kept_ref[2 * LANES :].astype(F32) + near_sum + far_sum


def combine(peers, cap, take_ref, got_ref, out_ref, wide_ref):
    wide_ref[...] = got_ref[...].astype(F32)
    rows = wide_ref.shape[0] // peers
    cols = rows // cap
    for c in range(cols):
        part = [wide_ref[pl.ds(j * cols + c, peers, stride=rows), :] for j in range(cap)]
        piece = jnp.concatenate(part, axis=0).astype(BF)
        total = jnp.dot(take_ref[...], piece, preferred_element_type=F32)
        out_ref[:, c * LANES : (c + 1) * LANES] = total.astype(BF)


ROLES = (4, 3, 1, -3, -1, 2, -2, 0)


def on_device(expert_ids, grad_hidden, stored_inputs, gate_weight, up_weight):
    peers = lax.axis_size("expert")
    replicas = lax.axis_size("dp")
    chips = replicas // 2
    cap, width = stored_inputs.shape[3], stored_inputs.shape[4]
    hidden = gate_weight.shape[2]
    tokens, picks = expert_ids.shape
    routed, slot_rows = tokens * picks, peers * cap
    sds = jax.ShapeDtypeStruct
    w_gate, w_up = gate_weight[0], up_weight[0]
    x = stored_inputs[0, 0].transpose(1, 0, 2).reshape(slot_rows, width)
    spot = lax.axis_index("dp")
    spot = jnp.stack([spot % 2, spot // 2]).astype(jnp.int32)

    def along_z(value, offset):
        pairs = []
        for z in range(chips):
            for core in range(2):
                to = (z + (offset if core == 0 else -offset)) % chips
                pairs.append((2 * z + core, 2 * to + core))
        return lax.ppermute(value, "dp", pairs)

    swap = functools.partial(lax.ppermute, axis_name="dp", perm=[(i, i ^ 1) for i in range(replicas)])

    in_rows = -(-(cap * hidden // LANES) // 8) * 8
    outgoing, take = call(
        functools.partial(pack, peers, cap),
        (sds((peers * in_rows, LANES), BF), sds((tokens, slot_rows), BF)),
        "hh",
        [pltpu.VMEM((peers * in_rows, LANES), F32)],
        flops=2 * slot_rows * routed * hidden,
        moved=4 * peers * in_rows * LANES,
    )(expert_ids.T, grad_hidden.reshape(routed, hidden))
    arrived = lax.all_to_all(outgoing.reshape(peers, in_rows, LANES), "expert", 0, 0, tiled=True)

    half = chips * LANES
    lent = call(partner_columns, sds((slot_rows, half), BF), "sh", moved=4 * slot_rows * half)(spot, x)
    borrowed = swap(lent)
    parts = hidden // 256
    f_gate, f_up = pl.pallas_call(
        factors,
        grid=(parts,),
        out_shape=(sds((slot_rows, hidden), F32),) * 2,
        in_specs=[
            pl.BlockSpec((slot_rows, width), lambda i: (0, 0)),
            pl.BlockSpec((width, 256), lambda i: (0, i)),
            pl.BlockSpec((width, 256), lambda i: (0, i)),
        ],
        out_specs=(pl.BlockSpec((slot_rows, 256), lambda i: (0, i)),) * 2,
        compiler_params=pltpu.CompilerParams(vmem_limit_bytes=24 * MIB),
        cost_estimate=pl.CostEstimate(
            flops=4 * slot_rows * width * hidden, bytes_accessed=8 * width * hidden, transcendentals=slot_rows * hidden
        ),
    )(far(x), far(w_gate), far(w_up))
    apart = -(-slot_rows // LANES) * LANES
    x_roles = call(
        functools.partial(by_role, ROLES),
        sds((len(ROLES) * LANES, 2 * apart), BF),
        "shv",
        moved=8 * slot_rows * half,
        near=True,
    )(spot, x, borrowed)

    dgate, dup = call(
        functools.partial(hidden_grads, peers, cap),
        (sds((slot_rows, hidden), BF),) * 2,
        "dddo",
        [pltpu.VMEM((peers * in_rows, LANES), F32)],
        moved=16 * slot_rows * hidden,
        near=True,
    )(arrived.reshape(peers * in_rows, LANES), f_gate, f_up, x_roles)
    dgate_near = swap(dgate)

    out_rows = cap * width // LANES
    steps = 8
    back = call(
        functools.partial(input_grads, peers, cap, steps),
        sds((peers * out_rows, LANES), BF),
        "vvuu",
        [
            pltpu.VMEM((peers * out_rows, LANES), F32),
            pltpu.VMEM((width, hidden), BF),
            pltpu.VMEM((width, hidden), BF),
            pltpu.SemaphoreType.DMA((2, steps)),
        ],
        flops=1,
        moved=1,
    )(dgate, dup, w_gate, w_up)
    returned = lax.all_to_all(back.reshape(peers, out_rows, LANES), "expert", 0, 0, tiled=True)

    blocks = [sds((n * LANES, hidden), BF) for n in (1, 2, 2, 3)]
    most, right, left, kept = call(
        partials, blocks, "vvvu", flops=20_000_000_000, moved=16 * LANES * hidden, near=True
    )(x_roles, dgate, dgate_near, back)
    left_in = along_z(left, -1)
    right_in = along_z(right, 1)
    most_in = along_z(most, 2)

    moved = 10 * LANES * hidden
    block = sds((LANES, hidden), BF)
    right_sum = along_z(call(sum_right, block, "vvv", flops=moved, moved=moved, near=True)(kept, right_in, most_in), 2)
    left_sum = along_z(call(sum_left, block, "vv", flops=moved, moved=moved, near=True)(kept, left_in), -2)
    grad_tokens = call(
        functools.partial(combine, peers, cap),
        sds((tokens, width), BF),
        "vv",
        [pltpu.VMEM((peers * out_rows, LANES), F32)],
        flops=1,
        moved=1,
    )(take, returned.reshape(peers * out_rows, LANES))
    grad_gate = call(sum_own, sds((LANES, hidden), F32), "vvvvvu", moved=2 * moved)(
        kept, right_in, left_in, right_sum, left_sum, grad_tokens
    )
    return (grad_tokens, grad_gate[None])


def solution(mesh):
    return jax.shard_map(
        on_device,
        mesh=mesh,
        in_specs=(
            P(("dp", "expert"), None),
            P(("dp", "expert"), None, None),
            P("dp", "expert", None, None, None),
            P("expert", None, None),
            P("expert", None, None),
        ),
        out_specs=(P(("dp", "expert"), None), P("expert", "dp", None)),
        check_vma=False,
    )
```

```python
import functools

import jax
import jax.numpy as jnp
from jax import lax
from jax.experimental import pallas as pl
from jax.experimental.pallas import tpu as pltpu
from jax.sharding import PartitionSpec as P

BF, F32 = jnp.bfloat16, jnp.float32
LANES = 128
MIB = 1 << 20
NT = (((1,), (1,)), ((), ()))


def call(body, outs, ins, scratch=(), flops=0, moved=0, near=False, vmem=16):
    specs = {"h": pl.BlockSpec(), "d": pl.BlockSpec(), "v": pl.BlockSpec(memory_space=pltpu.VMEM)}
    specs |= {"s": pl.BlockSpec(memory_space=pltpu.SMEM), "u": pl.BlockSpec(memory_space=pl.ANY), "o": pl.BlockSpec(memory_space=pl.ANY)}
    kernel = pl.pallas_call(
        body,
        out_shape=outs if near else jax.tree.map(lambda out: pltpu.HBM(out.shape, out.dtype), outs),
        in_specs=[specs[kind] for kind in ins],
        out_specs=jax.tree.map(lambda _: specs["v" if near else "h"], outs),
        scratch_shapes=list(scratch),
        compiler_params=pltpu.CompilerParams(vmem_limit_bytes=vmem * MIB),
        cost_estimate=pl.CostEstimate(flops=flops, bytes_accessed=moved, transcendentals=0),
    )
    return lambda *given: kernel(*(far(v) if kind in "hu" else v for kind, v in zip(ins, given)))


def far(value):
    return pltpu.with_memory_space_constraint(value, pltpu.HBM)


def iota(shape, axis):
    return lax.broadcasted_iota(jnp.int32, shape, axis)


def pack(peers, cap, ids_ref, grads_ref, out_ref, take_ref, wide_ref):
    picks, tokens = ids_ref.shape
    routed, hidden = grads_ref.shape
    ids = ids_ref[...].astype(F32).astype(BF)
    token_of = (iota((tokens, routed), 1) // picks == iota((tokens, routed), 0)).astype(F32).astype(BF)
    by_row = jnp.dot(ids, token_of, preferred_element_type=F32)
    mine = iota((picks, routed), 1) % picks == iota((picks, routed), 0)
    e_row = jnp.sum(jnp.where(mine, by_row, 0.0), axis=0, keepdims=True)
    token_col = (iota((routed, tokens), 0) // picks == iota((routed, tokens), 1)).astype(F32).astype(BF)
    by_col = lax.dot_general(token_col, ids, NT, preferred_element_type=F32)
    mine = iota((routed, picks), 0) % picks == iota((routed, picks), 1)
    e_col = jnp.sum(jnp.where(mine, by_col, 0.0), axis=1, keepdims=True)
    earlier = iota((routed, routed), 0) < iota((routed, routed), 1)
    slot = jnp.sum(jnp.where(earlier & (e_col == e_row), 1.0, 0.0), axis=0, keepdims=True)
    row = slot * peers + e_row
    place = (iota((cap * peers, routed), 0).astype(F32) == row).astype(F32).astype(BF)
    sent = jnp.dot(place, grads_ref[...], preferred_element_type=F32)
    cols = hidden // LANES
    rows = wide_ref.shape[0] // peers
    for j in range(cap):
        for c in range(cols):
            wide_ref[pl.ds(j * cols + c, peers, stride=rows), :] = sent[
                j * peers : (j + 1) * peers, c * LANES : (c + 1) * LANES
            ]
    for r in range(cap * cols, rows):
        wide_ref[pl.ds(r, peers, stride=rows), :] = jnp.zeros((peers, LANES), F32)
    out_ref[...] = wide_ref[...].astype(BF)
    take_ref[...] = lax.dot_general(token_of, place, NT, preferred_element_type=F32).astype(BF)


def partner_columns(core_ref, x_ref, out_ref):
    other = 1 - core_ref[0]
    for z in range(out_ref.shape[1] // LANES):
        start = pl.multiple_of((2 * z + other) * LANES, LANES)
        out_ref[:, z * LANES : (z + 1) * LANES] = x_ref[:, pl.ds(start, LANES)]


def by_role(roles, spot_ref, x_ref, partner_ref, out_ref):
    core, z = spot_ref[0], spot_ref[1]
    chips = partner_ref.shape[1] // LANES
    rows, apart = x_ref.shape[0], out_ref.shape[1] // 2
    sign = 1 - 2 * core
    for n, offset in zip(range(0, out_ref.shape[0], LANES), roles):
        chip = lax.rem(z + sign * offset + chips, chips)
        start = pl.multiple_of((2 * chip + core) * LANES, LANES)
        own = x_ref[:, pl.ds(start, LANES)].astype(F32)
        near = partner_ref[:, pl.ds(pl.multiple_of(chip * LANES, LANES), LANES)].astype(F32)
        out_ref[n : n + LANES, :rows] = own.T.astype(BF)
        out_ref[n : n + LANES, apart : apart + rows] = near.T.astype(BF)


def factors(x_ref, wg_ref, wu_ref, fg_ref, fu_ref, wg_kept, wu_kept):
    wg_kept[...] = wg_ref[: wg_kept.shape[0], :]
    wu_kept[...] = wu_ref[: wu_kept.shape[0], :]
    x = x_ref[...]
    gate = jnp.dot(x, wg_ref[...], preferred_element_type=F32)
    up = jnp.dot(x, wu_ref[...], preferred_element_type=F32)
    sig = 1.0 / (1.0 + jnp.exp(-gate))
    fg_ref[...] = up * sig * (1.0 + gate * (1.0 - sig))
    fu_ref[...] = gate * sig


def hidden_grads(peers, cap, got_ref, fg_ref, fu_ref, _, dgate_ref, dup_ref, wide_ref):
    wide_ref[...] = got_ref[...].astype(F32)
    rows = wide_ref.shape[0] // peers
    cols = fg_ref.shape[1] // LANES
    for j in range(cap):
        for c in range(cols):
            at = (slice(j * peers, (j + 1) * peers), slice(c * LANES, (c + 1) * LANES))
            piece = wide_ref[pl.ds(j * cols + c, peers, stride=rows), :]
            dgate_ref[at] = (piece * fg_ref[at]).astype(BF)
            dup_ref[at] = (piece * fu_ref[at]).astype(BF)


def input_grads(peers, cap, *refs):
    dgate_ref, dup_ref, wg_kept, wu_kept, wg_hbm, wu_hbm, out_ref, wide_ref, wg_ref, wu_ref, sems = refs
    width = wg_kept.shape[0]
    steps = wg_hbm.shape[0] // width
    copies = [
        [
            pltpu.make_async_copy(source.at[pl.ds(n * width, width)], held.at[n - 1], sems.at[i, n - 1])
            for i, (source, held) in enumerate(((wg_hbm, wg_ref), (wu_hbm, wu_ref)))
        ]
        for n in range(1, steps)
    ]

    def start(n):
        if n < steps:
            for copy in copies[n - 1]:
                copy.start()

    start(1)
    start(2)
    rows = wide_ref.shape[0] // peers
    cols = width // LANES
    for n in range(steps):
        if n > 0:
            for copy in copies[n - 1]:
                copy.wait()
            start(n + 2)
        wg, wu = (wg_kept[...], wu_kept[...]) if n == 0 else (wg_ref[n - 1], wu_ref[n - 1])
        back = lax.dot_general(dgate_ref[...], wg, NT, preferred_element_type=F32)
        back = back + lax.dot_general(dup_ref[...], wu, NT, preferred_element_type=F32)
        for j in range(cap):
            for c in range(cols):
                at = pl.ds(j * (rows // cap) + n * cols + c, peers, stride=rows)
                wide_ref[at, :] = back[j * peers : (j + 1) * peers, c * LANES : (c + 1) * LANES]
    out_ref[...] = wide_ref[...].astype(BF)


def partials(xt_ref, own_ref, near_ref, _, *outs):
    rows, apart = own_ref.shape[0], xt_ref.shape[1] // 2
    first = 0
    for out in outs:
        part = slice(first, first + out.shape[0])
        total = jnp.dot(xt_ref[part, :rows], own_ref[...], preferred_element_type=F32)
        total = total + jnp.dot(xt_ref[part, apart : apart + rows], near_ref[...], preferred_element_type=F32)
        out[...] = total.astype(BF)
        first += out.shape[0]


def sum_right(kept_ref, right_ref, most_ref, out_ref):
    far_sum = most_ref[...].astype(F32) + right_ref[...].astype(F32)
    out_ref[...] = (kept_ref[:LANES].astype(F32) + far_sum).astype(BF)


def sum_left(kept_ref, left_ref, out_ref):
    out_ref[...] = (kept_ref[LANES : 2 * LANES].astype(F32) + left_ref[...].astype(F32)).astype(BF)


def sum_own(kept_ref, right_ref, left_ref, right_sum_ref, left_sum_ref, _, out_ref):
    near_sum = right_ref[...].astype(F32) + left_ref[...].astype(F32)
    far_sum = right_sum_ref[...].astype(F32) + left_sum_ref[...].astype(F32)
    out_ref[...] = kept_ref[2 * LANES :].astype(F32) + near_sum + far_sum


def combine(peers, cap, take_ref, got_ref, out_ref, wide_ref):
    wide_ref[...] = got_ref[...].astype(F32)
    rows = wide_ref.shape[0] // peers
    cols = rows // cap
    for c in range(cols):
        part = [wide_ref[pl.ds(j * cols + c, peers, stride=rows), :] for j in range(cap)]
        piece = jnp.concatenate(part, axis=0).astype(BF)
        total = jnp.dot(take_ref[...], piece, preferred_element_type=F32)
        out_ref[:, c * LANES : (c + 1) * LANES] = total.astype(BF)


ROLES = (4, 3, -3, 1, -1, 2, -2, 0)


def on_device(expert_ids, grad_hidden, stored_inputs, gate_weight, up_weight):
    peers = lax.axis_size("expert")
    replicas = lax.axis_size("dp")
    chips = replicas // 2
    cap, width = stored_inputs.shape[3], stored_inputs.shape[4]
    hidden = gate_weight.shape[2]
    tokens, picks = expert_ids.shape
    routed, slot_rows = tokens * picks, peers * cap
    sds = jax.ShapeDtypeStruct
    w_gate, w_up = gate_weight[0], up_weight[0]
    x = stored_inputs[0, 0].transpose(1, 0, 2).reshape(slot_rows, width)
    spot = lax.axis_index("dp")
    spot = jnp.stack([spot % 2, spot // 2]).astype(jnp.int32)

    def along_z(value, offset):
        pairs = []
        for z in range(chips):
            for core in range(2):
                to = (z + (offset if core == 0 else -offset)) % chips
                pairs.append((2 * z + core, 2 * to + core))
        return lax.ppermute(value, "dp", pairs)

    swap = functools.partial(lax.ppermute, axis_name="dp", perm=[(i, i ^ 1) for i in range(replicas)])

    in_rows = -(-(cap * hidden // LANES) // 8) * 8
    outgoing, take = call(
        functools.partial(pack, peers, cap),
        (sds((peers * in_rows, LANES), BF), sds((tokens, slot_rows), BF)),
        "hh",
        [pltpu.VMEM((peers * in_rows, LANES), F32)],
        flops=2 * slot_rows * routed * hidden,
        moved=4 * peers * in_rows * LANES,
    )(expert_ids.T, grad_hidden.reshape(routed, hidden))
    arrived = lax.all_to_all(outgoing.reshape(peers, in_rows, LANES), "expert", 0, 0, tiled=True)

    half = chips * LANES
    lent = call(partner_columns, sds((slot_rows, half), BF), "sh", moved=4 * slot_rows * half)(spot, x)
    borrowed = swap(lent)
    parts = hidden // 256
    keep = width // 4
    f_gate, f_up, gate_kept, up_kept = pl.pallas_call(
        factors,
        grid=(parts,),
        out_shape=(sds((slot_rows, hidden), F32),) * 2 + (sds((keep, hidden), BF),) * 2,
        in_specs=[
            pl.BlockSpec((slot_rows, width), lambda i: (0, 0)),
            pl.BlockSpec((width, 256), lambda i: (0, i)),
            pl.BlockSpec((width, 256), lambda i: (0, i)),
        ],
        out_specs=(pl.BlockSpec((slot_rows, 256), lambda i: (0, i)),) * 2
        + (pl.BlockSpec((keep, 256), lambda i: (0, i)),) * 2,
        compiler_params=pltpu.CompilerParams(vmem_limit_bytes=24 * MIB),
        cost_estimate=pl.CostEstimate(
            flops=4 * slot_rows * width * hidden, bytes_accessed=8 * width * hidden, transcendentals=slot_rows * hidden
        ),
    )(far(x), far(w_gate), far(w_up))
    apart = -(-slot_rows // LANES) * LANES
    x_roles = call(
        functools.partial(by_role, ROLES),
        sds((len(ROLES) * LANES, 2 * apart), BF),
        "shv",
        moved=8 * slot_rows * half,
        near=False,
    )(spot, x, borrowed)

    dgate, dup = call(
        functools.partial(hidden_grads, peers, cap),
        (sds((slot_rows, hidden), BF),) * 2,
        "dddu",
        [pltpu.VMEM((peers * in_rows, LANES), F32)],
        moved=16 * slot_rows * hidden,
        near=True,
    )(arrived.reshape(peers * in_rows, LANES), f_gate, f_up, x_roles)
    dgate_near = swap(dgate)

    out_rows = cap * width // LANES
    back = call(
        functools.partial(input_grads, peers, cap),
        sds((peers * out_rows, LANES), BF),
        "vvvvuu",
        [
            pltpu.VMEM((peers * out_rows, LANES), F32),
            pltpu.VMEM((width // keep - 1, keep, hidden), BF),
            pltpu.VMEM((width // keep - 1, keep, hidden), BF),
            pltpu.SemaphoreType.DMA((2, width // keep - 1)),
        ],
        flops=1,
        moved=1,
    )(dgate, dup, gate_kept, up_kept, w_gate, w_up)
    returned = lax.all_to_all(back.reshape(peers, out_rows, LANES), "expert", 0, 0, tiled=True)

    blocks = [sds((n * LANES, hidden), BF) for n in (1, 1, 1, 1, 1, 3)]
    most, right, left, right_own, left_own, kept = call(
        partials, blocks, "hvdu", flops=20_000_000_000, moved=16 * LANES * hidden, near=True
    )(x_roles, dgate, dgate_near, back)
    most_in = along_z(most, 2)
    right_in = along_z(right, 1)
    left_in = along_z(left, -1)
    right_own_in = along_z(right_own, 1)
    left_own_in = along_z(left_own, -1)

    moved = 10 * LANES * hidden
    block = sds((LANES, hidden), BF)
    right_sum = along_z(call(sum_right, block, "vvv", flops=moved, moved=moved, near=True)(kept, right_in, most_in), 2)
    left_sum = along_z(call(sum_left, block, "vv", flops=moved, moved=moved, near=True)(kept, left_in), -2)
    grad_tokens = call(
        functools.partial(combine, peers, cap),
        sds((tokens, width), BF),
        "vv",
        [pltpu.VMEM((peers * out_rows, LANES), F32)],
        flops=1,
        moved=1,
    )(take, returned.reshape(peers * out_rows, LANES))
    grad_gate = call(sum_own, sds((LANES, hidden), F32), "vvvvvu", moved=2 * moved)(
        kept, right_own_in, left_own_in, right_sum, left_sum, grad_tokens
    )
    return (grad_tokens, grad_gate[None])


def solution(mesh):
    return jax.shard_map(
        on_device,
        mesh=mesh,
        in_specs=(
            P(("dp", "expert"), None),
            P(("dp", "expert"), None, None),
            P("dp", "expert", None, None, None),
            P("expert", None, None),
            P("expert", None, None),
        ),
        out_specs=(P(("dp", "expert"), None), P("expert", "dp", None)),
        check_vma=False,
    )
```

```python
import functools

import jax
import jax.numpy as jnp
from jax import lax
from jax.experimental import pallas as pl
from jax.experimental.pallas import tpu as pltpu
from jax.sharding import PartitionSpec as P

BF, F32 = jnp.bfloat16, jnp.float32
LANES = 128
MIB = 1 << 20
NT = (((1,), (1,)), ((), ()))


def call(body, outs, ins, scratch=(), flops=0, moved=0, near=False, vmem=16):
    specs = {"h": pl.BlockSpec(), "d": pl.BlockSpec(), "v": pl.BlockSpec(memory_space=pltpu.VMEM)}
    specs |= {"s": pl.BlockSpec(memory_space=pltpu.SMEM), "u": pl.BlockSpec(memory_space=pl.ANY), "o": pl.BlockSpec(memory_space=pl.ANY)}
    kernel = pl.pallas_call(
        body,
        out_shape=outs if near else jax.tree.map(lambda out: pltpu.HBM(out.shape, out.dtype), outs),
        in_specs=[specs[kind] for kind in ins],
        out_specs=jax.tree.map(lambda _: specs["v" if near else "h"], outs),
        scratch_shapes=list(scratch),
        compiler_params=pltpu.CompilerParams(vmem_limit_bytes=vmem * MIB),
        cost_estimate=pl.CostEstimate(flops=flops, bytes_accessed=moved, transcendentals=0),
    )
    return lambda *given: kernel(*(far(v) if kind in "hu" else v for kind, v in zip(ins, given)))


def far(value):
    return pltpu.with_memory_space_constraint(value, pltpu.HBM)


def iota(shape, axis):
    return lax.broadcasted_iota(jnp.int32, shape, axis)


def pack(peers, cap, ids_ref, grads_ref, out_ref, take_ref, wide_ref):
    picks, tokens = ids_ref.shape
    routed, hidden = grads_ref.shape
    ids = ids_ref[...].astype(F32).astype(BF)
    token_of = (iota((tokens, routed), 1) // picks == iota((tokens, routed), 0)).astype(F32).astype(BF)
    by_row = jnp.dot(ids, token_of, preferred_element_type=F32)
    mine = iota((picks, routed), 1) % picks == iota((picks, routed), 0)
    e_row = jnp.sum(jnp.where(mine, by_row, 0.0), axis=0, keepdims=True)
    token_col = (iota((routed, tokens), 0) // picks == iota((routed, tokens), 1)).astype(F32).astype(BF)
    by_col = lax.dot_general(token_col, ids, NT, preferred_element_type=F32)
    mine = iota((routed, picks), 0) % picks == iota((routed, picks), 1)
    e_col = jnp.sum(jnp.where(mine, by_col, 0.0), axis=1, keepdims=True)
    earlier = iota((routed, routed), 0) < iota((routed, routed), 1)
    slot = jnp.sum(jnp.where(earlier & (e_col == e_row), 1.0, 0.0), axis=0, keepdims=True)
    row = slot * peers + e_row
    place = (iota((cap * peers, routed), 0).astype(F32) == row).astype(F32).astype(BF)
    sent = jnp.dot(place, grads_ref[...], preferred_element_type=F32)
    cols = hidden // LANES
    rows = wide_ref.shape[0] // peers
    for j in range(cap):
        for c in range(cols):
            wide_ref[pl.ds(j * cols + c, peers, stride=rows), :] = sent[
                j * peers : (j + 1) * peers, c * LANES : (c + 1) * LANES
            ]
    for r in range(cap * cols, rows):
        wide_ref[pl.ds(r, peers, stride=rows), :] = jnp.zeros((peers, LANES), F32)
    out_ref[...] = wide_ref[...].astype(BF)
    take_ref[...] = lax.dot_general(token_of, place, NT, preferred_element_type=F32).astype(BF)


def partner_columns(core_ref, x_ref, out_ref):
    other = 1 - core_ref[0]
    for z in range(out_ref.shape[1] // LANES):
        start = pl.multiple_of((2 * z + other) * LANES, LANES)
        out_ref[:, z * LANES : (z + 1) * LANES] = x_ref[:, pl.ds(start, LANES)]


def by_role(roles, spot_ref, x_ref, partner_ref, out_ref):
    core, z = spot_ref[0], spot_ref[1]
    chips = partner_ref.shape[1] // LANES
    rows, apart = x_ref.shape[0], out_ref.shape[1] // 2
    sign = 1 - 2 * core
    for n, offset in zip(range(0, out_ref.shape[0], LANES), roles):
        chip = lax.rem(z + sign * offset + chips, chips)
        start = pl.multiple_of((2 * chip + core) * LANES, LANES)
        own = x_ref[:, pl.ds(start, LANES)].astype(F32)
        near = partner_ref[:, pl.ds(pl.multiple_of(chip * LANES, LANES), LANES)].astype(F32)
        out_ref[n : n + LANES, :rows] = own.T.astype(BF)
        out_ref[n : n + LANES, apart : apart + rows] = near.T.astype(BF)


def factors(x_ref, wg_ref, wu_ref, fg_ref, fu_ref, wg_kept, wu_kept):
    wg_kept[...] = wg_ref[: wg_kept.shape[0], :]
    wu_kept[...] = wu_ref[: wu_kept.shape[0], :]
    x = x_ref[...]
    gate = jnp.dot(x, wg_ref[...], preferred_element_type=F32)
    up = jnp.dot(x, wu_ref[...], preferred_element_type=F32)
    sig = 1.0 / (1.0 + jnp.exp(-gate))
    fg_ref[...] = up * sig * (1.0 + gate * (1.0 - sig))
    fu_ref[...] = gate * sig


def hidden_grads(peers, cap, got_ref, fg_ref, fu_ref, _, dgate_ref, dup_ref, wide_ref):
    wide_ref[...] = got_ref[...].astype(F32)
    rows = wide_ref.shape[0] // peers
    cols = fg_ref.shape[1] // LANES
    for j in range(cap):
        for c in range(cols):
            at = (slice(j * peers, (j + 1) * peers), slice(c * LANES, (c + 1) * LANES))
            piece = wide_ref[pl.ds(j * cols + c, peers, stride=rows), :]
            dgate_ref[at] = (piece * fg_ref[at]).astype(BF)
            dup_ref[at] = (piece * fu_ref[at]).astype(BF)


def input_grads(peers, cap, *refs):
    dgate_ref, dup_ref, wg_kept, wu_kept, wg_hbm, wu_hbm, out_ref, wide_ref, wg_ref, wu_ref, sems = refs
    width = wg_kept.shape[0]
    steps = wg_hbm.shape[0] // width
    copies = [
        [
            pltpu.make_async_copy(source.at[pl.ds(n * width, width)], held.at[n - 1], sems.at[i, n - 1])
            for i, (source, held) in enumerate(((wg_hbm, wg_ref), (wu_hbm, wu_ref)))
        ]
        for n in range(1, steps)
    ]

    def start(n):
        if n < steps:
            for copy in copies[n - 1]:
                copy.start()

    start(1)
    start(2)
    rows = wide_ref.shape[0] // peers
    cols = width // LANES
    for n in range(steps):
        if n > 0:
            for copy in copies[n - 1]:
                copy.wait()
            start(n + 2)
        wg, wu = (wg_kept[...], wu_kept[...]) if n == 0 else (wg_ref[n - 1], wu_ref[n - 1])
        back = lax.dot_general(dgate_ref[...], wg, NT, preferred_element_type=F32)
        back = back + lax.dot_general(dup_ref[...], wu, NT, preferred_element_type=F32)
        for j in range(cap):
            for c in range(cols):
                at = pl.ds(j * (rows // cap) + n * cols + c, peers, stride=rows)
                wide_ref[at, :] = back[j * peers : (j + 1) * peers, c * LANES : (c + 1) * LANES]
    out_ref[...] = wide_ref[...].astype(BF)


def tie(back_ref, _, out_ref):
    pass


def partials(xt_hbm, own_ref, near_ref, _, *refs):
    *outs, token_ref, xt_ref, sems = refs
    token_ref[...] = jnp.zeros_like(token_ref)
    rows, apart = own_ref.shape[0], xt_ref.shape[1] // 2
    places = [(out, n) for out in outs for n in range(0, out.shape[0], LANES)]
    copies = [
        pltpu.make_async_copy(
            xt_hbm.at[pl.ds(b * LANES, LANES)], xt_ref.at[pl.ds(b * LANES, LANES)], sems.at[b]
        )
        for b in range(len(places))
    ]
    for copy in copies[:3]:
        copy.start()
    for b, (out, n) in enumerate(places):
        copies[b].wait()
        if b + 3 < len(places):
            copies[b + 3].start()
        part = slice(b * LANES, (b + 1) * LANES)
        total = jnp.dot(xt_ref[part, :rows], own_ref[...], preferred_element_type=F32)
        total = total + jnp.dot(xt_ref[part, apart : apart + rows], near_ref[...], preferred_element_type=F32)
        out[n : n + LANES, :] = total.astype(BF)


def sum_right(kept_ref, most_ref, right_ref, out_ref):
    far_sum = most_ref[...].astype(F32) + right_ref[:LANES].astype(F32)
    out_ref[...] = (kept_ref[:LANES].astype(F32) + far_sum).astype(BF)


def sum_left(kept_ref, left_ref, out_ref):
    out_ref[...] = (kept_ref[LANES : 2 * LANES].astype(F32) + left_ref[:LANES].astype(F32)).astype(BF)


def sum_own(kept_ref, right_ref, left_ref, right_sum_ref, left_sum_ref, _, out_ref):
    near_sum = right_ref[LANES:].astype(F32) + left_ref[LANES:].astype(F32)
    far_sum = right_sum_ref[...].astype(F32) + left_sum_ref[...].astype(F32)
    out_ref[...] = kept_ref[2 * LANES :].astype(F32) + near_sum + far_sum


def combine(peers, cap, take_ref, got_ref, out_ref, wide_ref):
    wide_ref[...] = got_ref[...].astype(F32)
    rows = wide_ref.shape[0] // peers
    cols = rows // cap
    for c in range(cols):
        part = [wide_ref[pl.ds(j * cols + c, peers, stride=rows), :] for j in range(cap)]
        piece = jnp.concatenate(part, axis=0).astype(BF)
        total = jnp.dot(take_ref[...], piece, preferred_element_type=F32)
        out_ref[:, c * LANES : (c + 1) * LANES] = total.astype(BF)


ROLES = (4, 3, 1, -3, -1, 2, -2, 0)


def on_device(expert_ids, grad_hidden, stored_inputs, gate_weight, up_weight):
    peers = lax.axis_size("expert")
    replicas = lax.axis_size("dp")
    chips = replicas // 2
    cap, width = stored_inputs.shape[3], stored_inputs.shape[4]
    hidden = gate_weight.shape[2]
    tokens, picks = expert_ids.shape
    routed, slot_rows = tokens * picks, peers * cap
    sds = jax.ShapeDtypeStruct
    w_gate, w_up = gate_weight[0], up_weight[0]
    x = stored_inputs[0, 0].transpose(1, 0, 2).reshape(slot_rows, width)
    spot = lax.axis_index("dp")
    spot = jnp.stack([spot % 2, spot // 2]).astype(jnp.int32)

    def along_z(value, offset):
        pairs = []
        for z in range(chips):
            for core in range(2):
                to = (z + (offset if core == 0 else -offset)) % chips
                pairs.append((2 * z + core, 2 * to + core))
        return lax.ppermute(value, "dp", pairs)

    swap = functools.partial(lax.ppermute, axis_name="dp", perm=[(i, i ^ 1) for i in range(replicas)])

    in_rows = -(-(cap * hidden // LANES) // 8) * 8
    outgoing, take = call(
        functools.partial(pack, peers, cap),
        (sds((peers * in_rows, LANES), BF), sds((tokens, slot_rows), BF)),
        "hh",
        [pltpu.VMEM((peers * in_rows, LANES), F32)],
        flops=2 * slot_rows * routed * hidden,
        moved=4 * peers * in_rows * LANES,
    )(expert_ids.T, grad_hidden.reshape(routed, hidden))
    arrived = lax.all_to_all(outgoing.reshape(peers, in_rows, LANES), "expert", 0, 0, tiled=True)

    half = chips * LANES
    lent = call(partner_columns, sds((slot_rows, half), BF), "sh", moved=4 * slot_rows * half)(spot, x)
    borrowed = swap(lent)
    parts = hidden // 256
    keep = width // 4
    f_gate, f_up, gate_kept, up_kept = pl.pallas_call(
        factors,
        grid=(parts,),
        out_shape=(sds((slot_rows, hidden), F32),) * 2 + (sds((keep, hidden), BF),) * 2,
        in_specs=[
            pl.BlockSpec((slot_rows, width), lambda i: (0, 0)),
            pl.BlockSpec((width, 256), lambda i: (0, i)),
            pl.BlockSpec((width, 256), lambda i: (0, i)),
        ],
        out_specs=(pl.BlockSpec((slot_rows, 256), lambda i: (0, i)),) * 2
        + (pl.BlockSpec((keep, 256), lambda i: (0, i)),) * 2,
        compiler_params=pltpu.CompilerParams(vmem_limit_bytes=24 * MIB),
        cost_estimate=pl.CostEstimate(
            flops=4 * slot_rows * width * hidden, bytes_accessed=8 * width * hidden, transcendentals=slot_rows * hidden
        ),
    )(far(x), far(w_gate), far(w_up))
    apart = -(-slot_rows // LANES) * LANES
    x_roles = call(
        functools.partial(by_role, ROLES),
        sds((len(ROLES) * LANES, 2 * apart), BF),
        "shv",
        moved=8 * slot_rows * half,
        near=False,
    )(spot, x, borrowed)

    dgate, dup = call(
        functools.partial(hidden_grads, peers, cap),
        (sds((slot_rows, hidden), BF),) * 2,
        "dddu",
        [pltpu.VMEM((peers * in_rows, LANES), F32)],
        moved=16 * slot_rows * hidden,
        near=True,
    )(arrived.reshape(peers * in_rows, LANES), f_gate, f_up, x_roles)
    dgate_near = swap(dgate)

    out_rows = cap * width // LANES
    back = call(
        functools.partial(input_grads, peers, cap),
        sds((peers * out_rows, LANES), BF),
        "vvvvuu",
        [
            pltpu.VMEM((peers * out_rows, LANES), F32),
            pltpu.VMEM((width // keep - 1, keep, hidden), BF),
            pltpu.VMEM((width // keep - 1, keep, hidden), BF),
            pltpu.SemaphoreType.DMA((2, width // keep - 1)),
        ],
        flops=1,
        moved=1,
    )(dgate, dup, gate_kept, up_kept, w_gate, w_up)
    blocks = [sds((n * LANES, hidden), BF) for n in (1, 2, 2, 3)]
    most, right, left, kept, token = call(
        partials,
        blocks + [sds((8, LANES), F32)],
        "uvdu",
        [pltpu.VMEM((len(ROLES) * LANES, 2 * apart), BF), pltpu.SemaphoreType.DMA((len(ROLES),))],
        flops=1,
        moved=1,
        near=True,
    )(x_roles, dgate, dgate_near, back)
    back = pl.pallas_call(
        tie,
        out_shape=pltpu.HBM(back.shape, BF),
        in_specs=[pl.BlockSpec(memory_space=pl.ANY), pl.BlockSpec(memory_space=pltpu.VMEM)],
        out_specs=pl.BlockSpec(memory_space=pl.ANY),
        input_output_aliases={0: 0},
        cost_estimate=pl.CostEstimate(flops=1, bytes_accessed=1, transcendentals=0),
    )(far(back), token)
    returned = lax.all_to_all(back.reshape(peers, out_rows, LANES), "expert", 0, 0, tiled=True)

    most_in = along_z(most, 2)
    right_in = along_z(right, 1)
    left_in = along_z(left, -1)

    moved = 10 * LANES * hidden
    block = sds((LANES, hidden), BF)
    right_sum = call(sum_right, block, "vvv", flops=11_500_000_000, moved=moved, near=True)(kept, most_in, right_in)
    left_sum = call(sum_left, block, "vv", flops=1, moved=moved, near=True)(kept, left_in)
    right_sum = along_z(right_sum, 2)
    left_sum = along_z(left_sum, -2)
    grad_tokens = call(
        functools.partial(combine, peers, cap),
        sds((tokens, width), BF),
        "vv",
        [pltpu.VMEM((peers * out_rows, LANES), F32)],
        flops=1,
        moved=1,
    )(take, returned.reshape(peers * out_rows, LANES))
    grad_gate = call(sum_own, sds((LANES, hidden), F32), "vvvvvu", moved=2 * moved)(
        kept, right_in, left_in, right_sum, left_sum, grad_tokens
    )
    return (grad_tokens, grad_gate[None])


def solution(mesh):
    return jax.shard_map(
        on_device,
        mesh=mesh,
        in_specs=(
            P(("dp", "expert"), None),
            P(("dp", "expert"), None, None),
            P("dp", "expert", None, None, None),
            P("expert", None, None),
            P("expert", None, None),
        ),
        out_specs=(P(("dp", "expert"), None), P("expert", "dp", None)),
        check_vma=False,
    )
```

```python
import functools

import jax
import jax.numpy as jnp
from jax import lax
from jax.experimental import pallas as pl
from jax.experimental.pallas import tpu as pltpu
from jax.sharding import PartitionSpec as P

BF, F32 = jnp.bfloat16, jnp.float32
LANES = 128
MIB = 1 << 20
AHEAD = 3
NT = (((1,), (1,)), ((), ()))


def call(body, outs, ins, scratch=(), flops=0, moved=0, near=False, alias=None, vmem=16):
    specs = {"h": pl.BlockSpec(), "d": pl.BlockSpec(), "v": pl.BlockSpec(memory_space=pltpu.VMEM)}
    specs |= {"s": pl.BlockSpec(memory_space=pltpu.SMEM), "u": pl.BlockSpec(memory_space=pl.ANY), "o": pl.BlockSpec(memory_space=pl.ANY)}
    out_specs = jax.tree.map(lambda _: specs["v" if near else "h"], outs)
    if alias:
        ((source, place),) = alias.items()
        out_specs[place] = specs[ins[source]]
    kernel = pl.pallas_call(
        body,
        out_shape=outs if near else jax.tree.map(lambda out: pltpu.HBM(out.shape, out.dtype), outs),
        in_specs=[specs[kind] for kind in ins],
        out_specs=out_specs,
        input_output_aliases=alias or {},
        scratch_shapes=list(scratch),
        compiler_params=pltpu.CompilerParams(vmem_limit_bytes=vmem * MIB),
        cost_estimate=pl.CostEstimate(flops=flops, bytes_accessed=moved, transcendentals=0),
    )
    return lambda *given: kernel(*(far(v) if kind in "hu" else v for kind, v in zip(ins, given)))


def far(value):
    return pltpu.with_memory_space_constraint(value, pltpu.HBM)


def iota(shape, axis):
    return lax.broadcasted_iota(jnp.int32, shape, axis)


def pack(peers, cap, ids_ref, grads_ref, out_ref, take_ref, wide_ref):
    picks, tokens = ids_ref.shape
    routed, hidden = grads_ref.shape
    ids = ids_ref[...].astype(F32).astype(BF)
    token_of = (iota((tokens, routed), 1) // picks == iota((tokens, routed), 0)).astype(F32).astype(BF)
    by_row = jnp.dot(ids, token_of, preferred_element_type=F32)
    mine = iota((picks, routed), 1) % picks == iota((picks, routed), 0)
    e_row = jnp.sum(jnp.where(mine, by_row, 0.0), axis=0, keepdims=True)
    token_col = (iota((routed, tokens), 0) // picks == iota((routed, tokens), 1)).astype(F32).astype(BF)
    by_col = lax.dot_general(token_col, ids, NT, preferred_element_type=F32)
    mine = iota((routed, picks), 0) % picks == iota((routed, picks), 1)
    e_col = jnp.sum(jnp.where(mine, by_col, 0.0), axis=1, keepdims=True)
    earlier = iota((routed, routed), 0) < iota((routed, routed), 1)
    slot = jnp.sum(jnp.where(earlier & (e_col == e_row), 1.0, 0.0), axis=0, keepdims=True)
    row = slot * peers + e_row
    place = (iota((cap * peers, routed), 0).astype(F32) == row).astype(F32).astype(BF)
    sent = jnp.dot(place, grads_ref[...], preferred_element_type=F32)
    cols = hidden // LANES
    rows = wide_ref.shape[0] // peers
    for j in range(cap):
        for c in range(cols):
            wide_ref[pl.ds(j * cols + c, peers, stride=rows), :] = sent[
                j * peers : (j + 1) * peers, c * LANES : (c + 1) * LANES
            ]
    out_ref[...] = wide_ref[...].astype(BF)
    take_ref[...] = lax.dot_general(token_of, place, NT, preferred_element_type=F32).astype(BF)


def partner_columns(core_ref, x_ref, out_ref):
    other = 1 - core_ref[0]
    for z in range(out_ref.shape[1] // LANES):
        start = pl.multiple_of((2 * z + other) * LANES, LANES)
        out_ref[:, z * LANES : (z + 1) * LANES] = x_ref[:, pl.ds(start, LANES)]


def by_role(roles, spot_ref, x_ref, partner_ref, out_ref):
    core, z = spot_ref[0], spot_ref[1]
    chips = partner_ref.shape[1] // LANES
    rows, apart = x_ref.shape[0], out_ref.shape[1] // 2
    sign = 1 - 2 * core
    for n, offset in zip(range(0, out_ref.shape[0], LANES), roles):
        chip = lax.rem(z + sign * offset + chips, chips)
        start = pl.multiple_of((2 * chip + core) * LANES, LANES)
        own = x_ref[:, pl.ds(start, LANES)].astype(F32)
        near = partner_ref[:, pl.ds(pl.multiple_of(chip * LANES, LANES), LANES)].astype(F32)
        out_ref[n : n + LANES, :rows] = own.T.astype(BF)
        out_ref[n : n + LANES, apart : apart + rows] = near.T.astype(BF)


def factors(x_ref, wg_ref, wu_ref, fg_ref, fu_ref, wg_kept):
    wg_kept[...] = wg_ref[: wg_kept.shape[0], :]
    x = x_ref[...]
    gate = jnp.dot(x, wg_ref[...], preferred_element_type=F32)
    up = jnp.dot(x, wu_ref[...], preferred_element_type=F32)
    sig = 1.0 / (1.0 + jnp.exp(-gate))
    fg_ref[...] = up * sig * (1.0 + gate * (1.0 - sig))
    fu_ref[...] = gate * sig


def hidden_grads(peers, cap, got_ref, fg_ref, fu_ref, _, dgate_ref, dup_ref, wide_ref):
    wide_ref[...] = got_ref[...].astype(F32)
    rows = wide_ref.shape[0] // peers
    cols = fg_ref.shape[1] // LANES
    for j in range(cap):
        for c in range(cols):
            at = (slice(j * peers, (j + 1) * peers), slice(c * LANES, (c + 1) * LANES))
            piece = wide_ref[pl.ds(j * cols + c, peers, stride=rows), :]
            dgate_ref[at] = (piece * fg_ref[at]).astype(BF)
            dup_ref[at] = (piece * fu_ref[at]).astype(BF)


def input_grads(peers, cap, *refs):
    dgate_ref, dup_ref, wg_kept, wg_hbm, wu_hbm, out_ref, wide_ref, wg_ref, wu_ref, sems = refs
    width = wg_kept.shape[0]
    steps = wg_hbm.shape[0] // width
    copies = [
        [
            pltpu.make_async_copy(source.at[pl.ds(n * width, width)], held.at[n], sems.at[i, n])
            for i, (source, held) in enumerate(((wu_hbm, wu_ref), (wg_hbm, wg_ref)))
            if i == 0 or n > 0
        ]
        for n in range(steps)
    ]
    for pair in copies[:AHEAD]:
        for copy in pair:
            copy.start()
    rows = wide_ref.shape[0] // peers
    cols = width // LANES
    for n in range(steps):
        for copy in copies[n]:
            copy.wait()
        for copy in copies[n + AHEAD] if n + AHEAD < steps else ():
            copy.start()
        wg = wg_kept[...] if n == 0 else wg_ref[n]
        back = lax.dot_general(dgate_ref[...], wg, NT, preferred_element_type=F32)
        back = back + lax.dot_general(dup_ref[...], wu_ref[n], NT, preferred_element_type=F32)
        for j in range(cap):
            for c in range(cols):
                at = pl.ds(j * (rows // cap) + n * cols + c, peers, stride=rows)
                wide_ref[at, :] = back[j * peers : (j + 1) * peers, c * LANES : (c + 1) * LANES]
    out_ref[...] = wide_ref[...].astype(BF)


def partials(xt_ref, own_ref, near_ref, _, *refs):
    *outs, _ = refs
    rows, apart = own_ref.shape[0], xt_ref.shape[1] // 2
    first = 0
    for out in outs:
        part = slice(first, first + out.shape[0])
        total = jnp.dot(xt_ref[part, :rows], own_ref[...], preferred_element_type=F32)
        total = total + jnp.dot(xt_ref[part, apart : apart + rows], near_ref[...], preferred_element_type=F32)
        out[...] = total.astype(BF)
        first += out.shape[0]


def sum_most(kept_ref, most_ref, out_ref):
    out_ref[...] = kept_ref[:LANES].astype(F32) + most_ref[...].astype(F32)


def sum_right(part_ref, right_ref, out_ref):
    out_ref[...] = (part_ref[...] + right_ref[:LANES].astype(F32)).astype(BF)


def sum_left(kept_ref, left_ref, out_ref):
    out_ref[...] = (kept_ref[LANES : 2 * LANES].astype(F32) + left_ref[:LANES].astype(F32)).astype(BF)


def sum_own(kept_ref, right_ref, left_ref, right_sum_ref, left_sum_ref, _, out_ref):
    near_sum = right_ref[LANES:].astype(F32) + left_ref[LANES:].astype(F32)
    far_sum = right_sum_ref[...].astype(F32) + left_sum_ref[...].astype(F32)
    out_ref[...] = kept_ref[2 * LANES :].astype(F32) + near_sum + far_sum


def combine(peers, cap, take_ref, got_ref, out_ref, wide_ref):
    wide_ref[...] = got_ref[...].astype(F32)
    rows = wide_ref.shape[0] // peers
    cols = rows // cap
    for c in range(cols):
        part = [wide_ref[pl.ds(j * cols + c, peers, stride=rows), :] for j in range(cap)]
        piece = jnp.concatenate(part, axis=0).astype(BF)
        total = jnp.dot(take_ref[...], piece, preferred_element_type=F32)
        out_ref[:, c * LANES : (c + 1) * LANES] = total.astype(BF)


ROLES = (4, 3, 1, -3, -1, 2, -2, 0)


def on_device(expert_ids, grad_hidden, stored_inputs, gate_weight, up_weight):
    peers = lax.axis_size("expert")
    replicas = lax.axis_size("dp")
    chips = replicas // 2
    cap, width = stored_inputs.shape[3], stored_inputs.shape[4]
    hidden = gate_weight.shape[2]
    tokens, picks = expert_ids.shape
    routed, slot_rows = tokens * picks, peers * cap
    sds = jax.ShapeDtypeStruct
    w_gate, w_up = gate_weight[0], up_weight[0]
    x = stored_inputs[0, 0].transpose(1, 0, 2).reshape(slot_rows, width)
    spot = lax.axis_index("dp")
    spot = jnp.stack([spot % 2, spot // 2]).astype(jnp.int32)

    def along_z(value, offset):
        pairs = []
        for z in range(chips):
            for core in range(2):
                to = (z + (offset if core == 0 else -offset)) % chips
                pairs.append((2 * z + core, 2 * to + core))
        return lax.ppermute(value, "dp", pairs)

    swap = functools.partial(lax.ppermute, axis_name="dp", perm=[(i, i ^ 1) for i in range(replicas)])

    in_rows = -(-(cap * hidden // LANES) // 8) * 8
    outgoing, take = call(
        functools.partial(pack, peers, cap),
        (sds((peers * in_rows, LANES), BF), sds((tokens, slot_rows), BF)),
        "hh",
        [pltpu.VMEM((peers * in_rows, LANES), F32)],
        flops=2 * slot_rows * routed * hidden,
        moved=4 * peers * in_rows * LANES,
    )(expert_ids.T, grad_hidden.reshape(routed, hidden))
    arrived = lax.all_to_all(outgoing.reshape(peers, in_rows, LANES), "expert", 0, 0, tiled=True)

    half = chips * LANES
    lent = call(partner_columns, sds((slot_rows, half), BF), "sh", moved=4 * slot_rows * half)(spot, x)
    borrowed = swap(lent)
    parts = hidden // 256
    keep = width // 8
    f_gate, f_up, gate_kept = pl.pallas_call(
        factors,
        grid=(parts,),
        out_shape=(sds((slot_rows, hidden), F32),) * 2 + (sds((keep, hidden), BF),),
        in_specs=[
            pl.BlockSpec((slot_rows, width), lambda i: (0, 0)),
            pl.BlockSpec((width, 256), lambda i: (0, i)),
            pl.BlockSpec((width, 256), lambda i: (0, i)),
        ],
        out_specs=(pl.BlockSpec((slot_rows, 256), lambda i: (0, i)),) * 2
        + (pl.BlockSpec((keep, 256), lambda i: (0, i)),),
        compiler_params=pltpu.CompilerParams(vmem_limit_bytes=24 * MIB),
        cost_estimate=pl.CostEstimate(
            flops=4 * slot_rows * width * hidden, bytes_accessed=8 * width * hidden, transcendentals=slot_rows * hidden
        ),
    )(far(x), far(w_gate), far(w_up))
    apart = -(-slot_rows // LANES) * LANES
    x_roles = call(
        functools.partial(by_role, ROLES),
        sds((len(ROLES) * LANES, 2 * apart), BF),
        "shv",
        moved=8 * slot_rows * half,
        near=True,
    )(spot, x, borrowed)

    dgate, dup = call(
        functools.partial(hidden_grads, peers, cap),
        (sds((slot_rows, hidden), BF),) * 2,
        "dddo",
        [pltpu.VMEM((peers * in_rows, LANES), F32)],
        moved=16 * slot_rows * hidden,
        near=True,
    )(arrived.reshape(peers * in_rows, LANES), f_gate, f_up, x_roles)
    dgate_near = swap(dgate)

    out_rows = cap * width // LANES
    back = call(
        functools.partial(input_grads, peers, cap),
        sds((peers * out_rows, LANES), BF),
        "vvvuu",
        [
            pltpu.VMEM((peers * out_rows, LANES), F32),
            pltpu.VMEM((width // keep, keep, hidden), BF),
            pltpu.VMEM((width // keep, keep, hidden), BF),
            pltpu.SemaphoreType.DMA((2, width // keep)),
        ],
        flops=1,
        moved=1,
    )(dgate, dup, gate_kept, w_gate, w_up)
    blocks = [sds((n * LANES, hidden), BF) for n in (1, 2, 2, 3)]
    most, right, left, kept, back = call(
        partials,
        blocks + [pltpu.HBM(back.shape, BF)],
        "vvvu",
        flops=1,
        moved=1,
        near=True,
        alias={3: len(blocks)},
    )(x_roles, dgate, dgate_near, back)
    returned = lax.all_to_all(back.reshape(peers, out_rows, LANES), "expert", 0, 0, tiled=True)

    most_in = along_z(most, 2)
    right_in = along_z(right, 1)
    left_in = along_z(left, -1)

    moved = 10 * LANES * hidden
    block = sds((LANES, hidden), BF)
    part = call(sum_most, sds((LANES, hidden), F32), "vv", flops=5_000_000_000, moved=moved, near=True)(kept, most_in)
    right_sum = call(sum_right, block, "vv", flops=10_500_000_000, moved=moved, near=True)(part, right_in)
    left_sum = call(sum_left, block, "vv", flops=1, moved=moved, near=True)(kept, left_in)
    right_sum = along_z(right_sum, 2)
    left_sum = along_z(left_sum, -2)
    grad_tokens = call(
        functools.partial(combine, peers, cap),
        sds((tokens, width), BF),
        "vv",
        [pltpu.VMEM((peers * out_rows, LANES), F32)],
        flops=1,
        moved=1,
    )(take, returned.reshape(peers * out_rows, LANES))
    grad_gate = call(sum_own, sds((LANES, hidden), F32), "vvvvvu", moved=2 * moved)(
        kept, right_in, left_in, right_sum, left_sum, grad_tokens
    )
    return (grad_tokens, grad_gate[None])


def solution(mesh):
    return jax.shard_map(
        on_device,
        mesh=mesh,
        in_specs=(
            P(("dp", "expert"), None),
            P(("dp", "expert"), None, None),
            P("dp", "expert", None, None, None),
            P("expert", None, None),
            P("expert", None, None),
        ),
        out_specs=(P(("dp", "expert"), None), P("expert", "dp", None)),
        check_vma=False,
    )
```

```python
import functools

import jax
import jax.numpy as jnp
from jax import lax
from jax.experimental import pallas as pl
from jax.experimental.pallas import tpu as pltpu
from jax.sharding import PartitionSpec as P

BF, F32 = jnp.bfloat16, jnp.float32
LANES = 128
MIB = 1 << 20
AHEAD = 2
NT = (((1,), (1,)), ((), ()))


def call(body, outs, ins, scratch=(), flops=0, moved=0, near=False, alias=None, vmem=16):
    specs = {"h": pl.BlockSpec(), "d": pl.BlockSpec(), "v": pl.BlockSpec(memory_space=pltpu.VMEM)}
    specs |= {"s": pl.BlockSpec(memory_space=pltpu.SMEM), "u": pl.BlockSpec(memory_space=pl.ANY), "o": pl.BlockSpec(memory_space=pl.ANY)}
    out_specs = jax.tree.map(lambda _: specs["v" if near else "h"], outs)
    if alias:
        ((source, place),) = alias.items()
        out_specs[place] = specs[ins[source]]
    kernel = pl.pallas_call(
        body,
        out_shape=outs if near else jax.tree.map(lambda out: pltpu.HBM(out.shape, out.dtype), outs),
        in_specs=[specs[kind] for kind in ins],
        out_specs=out_specs,
        input_output_aliases=alias or {},
        scratch_shapes=list(scratch),
        compiler_params=pltpu.CompilerParams(vmem_limit_bytes=vmem * MIB),
        cost_estimate=pl.CostEstimate(flops=flops, bytes_accessed=moved, transcendentals=0),
    )
    return lambda *given: kernel(*(far(v) if kind in "hu" else v for kind, v in zip(ins, given)))


def far(value):
    return pltpu.with_memory_space_constraint(value, pltpu.HBM)


def iota(shape, axis):
    return lax.broadcasted_iota(jnp.int32, shape, axis)


def pack(peers, cap, ids_ref, grads_ref, out_ref, take_ref, wide_ref):
    picks, tokens = ids_ref.shape
    routed, hidden = grads_ref.shape
    ids = ids_ref[...].astype(F32).astype(BF)
    token_of = (iota((tokens, routed), 1) // picks == iota((tokens, routed), 0)).astype(F32).astype(BF)
    by_row = jnp.dot(ids, token_of, preferred_element_type=F32)
    mine = iota((picks, routed), 1) % picks == iota((picks, routed), 0)
    e_row = jnp.sum(jnp.where(mine, by_row, 0.0), axis=0, keepdims=True)
    token_col = (iota((routed, tokens), 0) // picks == iota((routed, tokens), 1)).astype(F32).astype(BF)
    by_col = lax.dot_general(token_col, ids, NT, preferred_element_type=F32)
    mine = iota((routed, picks), 0) % picks == iota((routed, picks), 1)
    e_col = jnp.sum(jnp.where(mine, by_col, 0.0), axis=1, keepdims=True)
    earlier = iota((routed, routed), 0) < iota((routed, routed), 1)
    slot = jnp.sum(jnp.where(earlier & (e_col == e_row), 1.0, 0.0), axis=0, keepdims=True)
    row = slot * peers + e_row
    place = (iota((cap * peers, routed), 0).astype(F32) == row).astype(F32).astype(BF)
    sent = jnp.dot(place, grads_ref[...], preferred_element_type=F32)
    cols = hidden // LANES
    rows = wide_ref.shape[0] // peers
    for j in range(cap):
        for c in range(cols):
            wide_ref[pl.ds(j * cols + c, peers, stride=rows), :] = sent[
                j * peers : (j + 1) * peers, c * LANES : (c + 1) * LANES
            ]
    out_ref[...] = wide_ref[...].astype(BF)
    take_ref[...] = lax.dot_general(token_of, place, NT, preferred_element_type=F32).astype(BF)


def partner_columns(core_ref, x_ref, out_ref):
    other = 1 - core_ref[0]
    for z in range(out_ref.shape[1] // LANES):
        start = pl.multiple_of((2 * z + other) * LANES, LANES)
        out_ref[:, z * LANES : (z + 1) * LANES] = x_ref[:, pl.ds(start, LANES)]


def by_role(roles, spot_ref, x_ref, partner_ref, out_ref):
    core, z = spot_ref[0], spot_ref[1]
    chips = partner_ref.shape[1] // LANES
    rows, apart = x_ref.shape[0], out_ref.shape[1] // 2
    sign = 1 - 2 * core
    for n, offset in zip(range(0, out_ref.shape[0], LANES), roles):
        chip = lax.rem(z + sign * offset + chips, chips)
        start = pl.multiple_of((2 * chip + core) * LANES, LANES)
        own = x_ref[:, pl.ds(start, LANES)].astype(F32)
        near = partner_ref[:, pl.ds(pl.multiple_of(chip * LANES, LANES), LANES)].astype(F32)
        out_ref[n : n + LANES, :rows] = own.T.astype(BF)
        out_ref[n : n + LANES, apart : apart + rows] = near.T.astype(BF)


def factors(x_ref, wg_ref, wu_ref, fg_ref, fu_ref):
    x = x_ref[...]
    gate = jnp.dot(x, wg_ref[...], preferred_element_type=F32)
    up = jnp.dot(x, wu_ref[...], preferred_element_type=F32)
    sig = 1.0 / (1.0 + jnp.exp(-gate))
    fg_ref[...] = up * sig * (1.0 + gate * (1.0 - sig))
    fu_ref[...] = gate * sig


def hidden_grads(peers, cap, got_ref, fg_ref, fu_ref, _, dgate_ref, dup_ref, wide_ref):
    wide_ref[...] = got_ref[...].astype(F32)
    rows = wide_ref.shape[0] // peers
    cols = fg_ref.shape[1] // LANES
    for j in range(cap):
        for c in range(cols):
            at = (slice(j * peers, (j + 1) * peers), slice(c * LANES, (c + 1) * LANES))
            piece = wide_ref[pl.ds(j * cols + c, peers, stride=rows), :]
            dgate_ref[at] = (piece * fg_ref[at]).astype(BF)
            dup_ref[at] = (piece * fu_ref[at]).astype(BF)


def input_grads(peers, cap, *refs):
    dgate_ref, dup_ref, wg_hbm, wu_hbm, out_ref, wide_ref, wg_ref, wu_ref, sems = refs
    steps, width, _ = wg_ref.shape
    copies = [
        [
            pltpu.make_async_copy(source.at[pl.ds(n * width, width)], held.at[n], sems.at[i, n])
            for i, (source, held) in enumerate(((wg_hbm, wg_ref), (wu_hbm, wu_ref)))
        ]
        for n in range(steps)
    ]
    for pair in copies[:AHEAD]:
        for copy in pair:
            copy.start()
    rows = wide_ref.shape[0] // peers
    cols = width // LANES
    for n in range(steps):
        for copy in copies[n]:
            copy.wait()
        for copy in copies[n + AHEAD] if n + AHEAD < steps else ():
            copy.start()
        back = lax.dot_general(dgate_ref[...], wg_ref[n], NT, preferred_element_type=F32)
        back = back + lax.dot_general(dup_ref[...], wu_ref[n], NT, preferred_element_type=F32)
        for j in range(cap):
            for c in range(cols):
                at = pl.ds(j * (rows // cap) + n * cols + c, peers, stride=rows)
                wide_ref[at, :] = back[j * peers : (j + 1) * peers, c * LANES : (c + 1) * LANES]
    out_ref[...] = wide_ref[...].astype(BF)


def partials(xt_ref, own_ref, near_ref, _, *refs):
    *outs, _ = refs
    rows, apart = own_ref.shape[0], xt_ref.shape[1] // 2
    first = 0
    for out in outs:
        part = slice(first, first + out.shape[0])
        total = jnp.dot(xt_ref[part, :rows], own_ref[...], preferred_element_type=F32)
        total = total + jnp.dot(xt_ref[part, apart : apart + rows], near_ref[...], preferred_element_type=F32)
        out[...] = total.astype(BF)
        first += out.shape[0]


def sum_most(kept_ref, most_ref, out_ref):
    out_ref[...] = kept_ref[:LANES].astype(F32) + most_ref[...].astype(F32)


def sum_right(part_ref, right_ref, out_ref):
    out_ref[...] = (part_ref[...] + right_ref[...].astype(F32)).astype(BF)


def sum_left(kept_ref, left_ref, out_ref):
    out_ref[...] = (kept_ref[LANES : 2 * LANES].astype(F32) + left_ref[...].astype(F32)).astype(BF)


def sum_own(kept_ref, right_ref, left_ref, right_sum_ref, left_sum_ref, _, out_ref):
    near_sum = right_ref[...].astype(F32) + left_ref[...].astype(F32)
    far_sum = right_sum_ref[...].astype(F32) + left_sum_ref[...].astype(F32)
    out_ref[...] = kept_ref[2 * LANES :].astype(F32) + near_sum + far_sum


def combine(peers, cap, take_ref, got_ref, out_ref, wide_ref):
    wide_ref[...] = got_ref[...].astype(F32)
    rows = wide_ref.shape[0] // peers
    cols = rows // cap
    for c in range(cols):
        part = [wide_ref[pl.ds(j * cols + c, peers, stride=rows), :] for j in range(cap)]
        piece = jnp.concatenate(part, axis=0).astype(BF)
        total = jnp.dot(take_ref[...], piece, preferred_element_type=F32)
        out_ref[:, c * LANES : (c + 1) * LANES] = total.astype(BF)


ROLES = (4, 3, -3, 1, -1, 2, -2, 0)


def on_device(expert_ids, grad_hidden, stored_inputs, gate_weight, up_weight):
    peers = lax.axis_size("expert")
    replicas = lax.axis_size("dp")
    chips = replicas // 2
    cap, width = stored_inputs.shape[3], stored_inputs.shape[4]
    hidden = gate_weight.shape[2]
    tokens, picks = expert_ids.shape
    routed, slot_rows = tokens * picks, peers * cap
    sds = jax.ShapeDtypeStruct
    w_gate, w_up = gate_weight[0], up_weight[0]
    x = stored_inputs[0, 0].transpose(1, 0, 2).reshape(slot_rows, width)
    spot = lax.axis_index("dp")
    spot = jnp.stack([spot % 2, spot // 2]).astype(jnp.int32)

    def along_z(value, offset):
        pairs = []
        for z in range(chips):
            for core in range(2):
                to = (z + (offset if core == 0 else -offset)) % chips
                pairs.append((2 * z + core, 2 * to + core))
        return lax.ppermute(value, "dp", pairs)

    swap = functools.partial(lax.ppermute, axis_name="dp", perm=[(i, i ^ 1) for i in range(replicas)])

    in_rows = -(-(cap * hidden // LANES) // 8) * 8
    outgoing, take = call(
        functools.partial(pack, peers, cap),
        (sds((peers * in_rows, LANES), BF), sds((tokens, slot_rows), BF)),
        "hh",
        [pltpu.VMEM((peers * in_rows, LANES), F32)],
        flops=2 * slot_rows * routed * hidden,
        moved=4 * peers * in_rows * LANES,
    )(expert_ids.T, grad_hidden.reshape(routed, hidden))
    arrived = lax.all_to_all(outgoing.reshape(peers, in_rows, LANES), "expert", 0, 0, tiled=True)

    half = chips * LANES
    lent = call(partner_columns, sds((slot_rows, half), BF), "sh", moved=4 * slot_rows * half)(spot, x)
    borrowed = swap(lent)
    parts = hidden // 256
    f_gate, f_up = pl.pallas_call(
        factors,
        grid=(parts,),
        out_shape=(sds((slot_rows, hidden), F32),) * 2,
        in_specs=[
            pl.BlockSpec((slot_rows, width), lambda i: (0, 0)),
            pl.BlockSpec((width, 256), lambda i: (0, i)),
            pl.BlockSpec((width, 256), lambda i: (0, i)),
        ],
        out_specs=(pl.BlockSpec((slot_rows, 256), lambda i: (0, i)),) * 2,
        compiler_params=pltpu.CompilerParams(vmem_limit_bytes=24 * MIB),
        cost_estimate=pl.CostEstimate(
            flops=4 * slot_rows * width * hidden, bytes_accessed=8 * width * hidden, transcendentals=slot_rows * hidden
        ),
    )(far(x), far(w_gate), far(w_up))
    apart = -(-slot_rows // LANES) * LANES
    x_roles = call(
        functools.partial(by_role, ROLES),
        sds((len(ROLES) * LANES, 2 * apart), BF),
        "shv",
        moved=8 * slot_rows * half,
        near=True,
    )(spot, x, borrowed)

    dgate, dup = call(
        functools.partial(hidden_grads, peers, cap),
        (sds((slot_rows, hidden), BF),) * 2,
        "dddo",
        [pltpu.VMEM((peers * in_rows, LANES), F32)],
        moved=16 * slot_rows * hidden,
        near=True,
    )(arrived.reshape(peers * in_rows, LANES), f_gate, f_up, x_roles)
    dgate_near = swap(dgate)

    out_rows, steps = cap * width // LANES, 4
    back = call(
        functools.partial(input_grads, peers, cap),
        sds((peers * out_rows, LANES), BF),
        "vvuu",
        [
            pltpu.VMEM((peers * out_rows, LANES), F32),
            pltpu.VMEM((steps, width // steps, hidden), BF),
            pltpu.VMEM((steps, width // steps, hidden), BF),
            pltpu.SemaphoreType.DMA((2, steps)),
        ],
        flops=1,
        moved=1,
    )(dgate, dup, w_gate, w_up)
    blocks = [sds((n * LANES, hidden), BF) for n in (1, 1, 1, 1, 1, 3)]
    most, right, left, right_own, left_own, kept, back = call(
        partials,
        blocks + [pltpu.HBM(back.shape, BF)],
        "vvvu",
        flops=1,
        moved=1,
        near=True,
        alias={3: len(blocks)},
    )(x_roles, dgate, dgate_near, back)
    returned = lax.all_to_all(back.reshape(peers, out_rows, LANES), "expert", 0, 0, tiled=True)

    most_in = along_z(most, 2)
    right_in = along_z(right, 1)
    left_in = along_z(left, -1)
    right_own_in = along_z(right_own, 1)
    left_own_in = along_z(left_own, -1)

    moved = 10 * LANES * hidden
    block = sds((LANES, hidden), BF)
    part = call(sum_most, sds((LANES, hidden), F32), "vv", flops=5_000_000_000, moved=moved, near=True)(kept, most_in)
    right_sum = call(sum_right, block, "vv", flops=10_500_000_000, moved=moved, near=True)(part, right_in)
    left_sum = call(sum_left, block, "vv", flops=1, moved=moved, near=True)(kept, left_in)
    right_sum = along_z(right_sum, 2)
    left_sum = along_z(left_sum, -2)
    grad_tokens = call(
        functools.partial(combine, peers, cap),
        sds((tokens, width), BF),
        "vv",
        [pltpu.VMEM((peers * out_rows, LANES), F32)],
        flops=1,
        moved=1,
    )(take, returned.reshape(peers * out_rows, LANES))
    grad_gate = call(sum_own, sds((LANES, hidden), F32), "vvvvvu", moved=2 * moved)(
        kept, right_own_in, left_own_in, right_sum, left_sum, grad_tokens
    )
    return (grad_tokens, grad_gate[None])


def solution(mesh):
    return jax.shard_map(
        on_device,
        mesh=mesh,
        in_specs=(
            P(("dp", "expert"), None),
            P(("dp", "expert"), None, None),
            P("dp", "expert", None, None, None),
            P("expert", None, None),
            P("expert", None, None),
        ),
        out_specs=(P(("dp", "expert"), None), P("expert", "dp", None)),
        check_vma=False,
    )
```

```python
import functools

import jax
import jax.numpy as jnp
from jax import lax
from jax.experimental import pallas as pl
from jax.experimental.pallas import tpu as pltpu
from jax.sharding import PartitionSpec as P

BF, F32 = jnp.bfloat16, jnp.float32
LANES = 128
MIB = 1 << 20
AHEAD = 2
NT = (((1,), (1,)), ((), ()))


def call(body, outs, ins, scratch=(), flops=0, moved=0, near=False, alias=None, vmem=16):
    specs = {"h": pl.BlockSpec(), "d": pl.BlockSpec(), "v": pl.BlockSpec(memory_space=pltpu.VMEM)}
    specs |= {"s": pl.BlockSpec(memory_space=pltpu.SMEM), "u": pl.BlockSpec(memory_space=pl.ANY), "o": pl.BlockSpec(memory_space=pl.ANY)}
    out_specs = jax.tree.map(lambda _: specs["v" if near else "h"], outs)
    if alias:
        ((source, place),) = alias.items()
        out_specs[place] = specs[ins[source]]
    kernel = pl.pallas_call(
        body,
        out_shape=outs if near else jax.tree.map(lambda out: pltpu.HBM(out.shape, out.dtype), outs),
        in_specs=[specs[kind] for kind in ins],
        out_specs=out_specs,
        input_output_aliases=alias or {},
        scratch_shapes=list(scratch),
        compiler_params=pltpu.CompilerParams(vmem_limit_bytes=vmem * MIB),
        cost_estimate=pl.CostEstimate(flops=flops, bytes_accessed=moved, transcendentals=0),
    )
    return lambda *given: kernel(*(far(v) if kind in "hu" else v for kind, v in zip(ins, given)))


def far(value):
    return pltpu.with_memory_space_constraint(value, pltpu.HBM)


def iota(shape, axis):
    return lax.broadcasted_iota(jnp.int32, shape, axis)


def pack(peers, cap, ids_ref, grads_ref, out_ref, take_ref, wide_ref):
    picks, tokens = ids_ref.shape
    routed, hidden = grads_ref.shape
    ids = ids_ref[...].astype(F32).astype(BF)
    token_of = (iota((tokens, routed), 1) // picks == iota((tokens, routed), 0)).astype(F32).astype(BF)
    by_row = jnp.dot(ids, token_of, preferred_element_type=F32)
    mine = iota((picks, routed), 1) % picks == iota((picks, routed), 0)
    e_row = jnp.sum(jnp.where(mine, by_row, 0.0), axis=0, keepdims=True)
    token_col = (iota((routed, tokens), 0) // picks == iota((routed, tokens), 1)).astype(F32).astype(BF)
    by_col = lax.dot_general(token_col, ids, NT, preferred_element_type=F32)
    mine = iota((routed, picks), 0) % picks == iota((routed, picks), 1)
    e_col = jnp.sum(jnp.where(mine, by_col, 0.0), axis=1, keepdims=True)
    earlier = iota((routed, routed), 0) < iota((routed, routed), 1)
    slot = jnp.sum(jnp.where(earlier & (e_col == e_row), 1.0, 0.0), axis=0, keepdims=True)
    row = slot * peers + e_row
    place = (iota((cap * peers, routed), 0).astype(F32) == row).astype(F32).astype(BF)
    sent = jnp.dot(place, grads_ref[...], preferred_element_type=F32)
    cols = hidden // LANES
    rows = wide_ref.shape[0] // peers
    for j in range(cap):
        for c in range(cols):
            wide_ref[pl.ds(j * cols + c, peers, stride=rows), :] = sent[
                j * peers : (j + 1) * peers, c * LANES : (c + 1) * LANES
            ]
    out_ref[...] = wide_ref[...].astype(BF)
    take_ref[...] = lax.dot_general(token_of, place, NT, preferred_element_type=F32).astype(BF)


def partner_columns(core_ref, x_ref, out_ref):
    other = 1 - core_ref[0]
    for z in range(out_ref.shape[1] // LANES):
        start = pl.multiple_of((2 * z + other) * LANES, LANES)
        out_ref[:, z * LANES : (z + 1) * LANES] = x_ref[:, pl.ds(start, LANES)]


def by_role(roles, spot_ref, x_ref, partner_ref, out_ref):
    core, z = spot_ref[0], spot_ref[1]
    chips = partner_ref.shape[1] // LANES
    rows, apart = x_ref.shape[0], out_ref.shape[1] // 2
    sign = 1 - 2 * core
    for n, offset in zip(range(0, out_ref.shape[0], LANES), roles):
        chip = lax.rem(z + sign * offset + chips, chips)
        start = pl.multiple_of((2 * chip + core) * LANES, LANES)
        own = x_ref[:, pl.ds(start, LANES)].astype(F32)
        near = partner_ref[:, pl.ds(pl.multiple_of(chip * LANES, LANES), LANES)].astype(F32)
        out_ref[n : n + LANES, :rows] = own.T.astype(BF)
        out_ref[n : n + LANES, apart : apart + rows] = near.T.astype(BF)


def factors(x_ref, wg_ref, wu_ref, fg_ref, fu_ref):
    x = x_ref[...]
    gate = jnp.dot(x, wg_ref[...], preferred_element_type=F32)
    up = jnp.dot(x, wu_ref[...], preferred_element_type=F32)
    sig = 1.0 / (1.0 + jnp.exp(-gate))
    fg_ref[...] = up * sig * (1.0 + gate * (1.0 - sig))
    fu_ref[...] = gate * sig


def hidden_grads(peers, cap, got_ref, fg_ref, fu_ref, _, dgate_ref, dup_ref, wide_ref):
    wide_ref[...] = got_ref[...].astype(F32)
    rows = wide_ref.shape[0] // peers
    cols = fg_ref.shape[1] // LANES
    for j in range(cap):
        for c in range(cols):
            at = (slice(j * peers, (j + 1) * peers), slice(c * LANES, (c + 1) * LANES))
            piece = wide_ref[pl.ds(j * cols + c, peers, stride=rows), :]
            dgate_ref[at] = (piece * fg_ref[at]).astype(BF)
            dup_ref[at] = (piece * fu_ref[at]).astype(BF)


def input_grads(peers, cap, *refs):
    dgate_ref, dup_ref, wg_hbm, wu_hbm, out_ref, wide_ref, wg_ref, wu_ref, sems = refs
    steps, width, _ = wg_ref.shape
    copies = [
        [
            pltpu.make_async_copy(source.at[pl.ds(n * width, width)], held.at[n], sems.at[i, n])
            for i, (source, held) in enumerate(((wg_hbm, wg_ref), (wu_hbm, wu_ref)))
        ]
        for n in range(steps)
    ]
    for pair in copies[:AHEAD]:
        for copy in pair:
            copy.start()
    rows = wide_ref.shape[0] // peers
    cols = width // LANES
    for n in range(steps):
        for copy in copies[n]:
            copy.wait()
        for copy in copies[n + AHEAD] if n + AHEAD < steps else ():
            copy.start()
        back = lax.dot_general(dgate_ref[...], wg_ref[n], NT, preferred_element_type=F32)
        back = back + lax.dot_general(dup_ref[...], wu_ref[n], NT, preferred_element_type=F32)
        for j in range(cap):
            for c in range(cols):
                at = pl.ds(j * (rows // cap) + n * cols + c, peers, stride=rows)
                wide_ref[at, :] = back[j * peers : (j + 1) * peers, c * LANES : (c + 1) * LANES]
    out_ref[...] = wide_ref[...].astype(BF)


def partials(xt_ref, own_ref, near_ref, _, *refs):
    *outs, _ = refs
    rows, apart = own_ref.shape[0], xt_ref.shape[1] // 2
    first = 0
    for out in outs:
        part = slice(first, first + out.shape[0])
        total = jnp.dot(xt_ref[part, :rows], own_ref[...], preferred_element_type=F32)
        total = total + jnp.dot(xt_ref[part, apart : apart + rows], near_ref[...], preferred_element_type=F32)
        out[...] = total.astype(BF)
        first += out.shape[0]


def sum_most(kept_ref, most_ref, out_ref):
    out_ref[...] = kept_ref[:LANES].astype(F32) + most_ref[...].astype(F32)


def sum_right(part_ref, right_ref, out_ref):
    out_ref[...] = (part_ref[...] + right_ref[:LANES].astype(F32)).astype(BF)


def sum_left(kept_ref, left_ref, out_ref):
    out_ref[...] = (kept_ref[LANES : 2 * LANES].astype(F32) + left_ref[:LANES].astype(F32)).astype(BF)


def sum_own(kept_ref, right_ref, left_ref, right_sum_ref, left_sum_ref, _, out_ref):
    near_sum = right_ref[LANES:].astype(F32) + left_ref[LANES:].astype(F32)
    far_sum = right_sum_ref[...].astype(F32) + left_sum_ref[...].astype(F32)
    out_ref[...] = kept_ref[2 * LANES :].astype(F32) + near_sum + far_sum


def combine(peers, cap, take_ref, got_ref, out_ref, wide_ref):
    wide_ref[...] = got_ref[...].astype(F32)
    rows = wide_ref.shape[0] // peers
    cols = rows // cap
    for c in range(cols):
        part = [wide_ref[pl.ds(j * cols + c, peers, stride=rows), :] for j in range(cap)]
        piece = jnp.concatenate(part, axis=0).astype(BF)
        total = jnp.dot(take_ref[...], piece, preferred_element_type=F32)
        out_ref[:, c * LANES : (c + 1) * LANES] = total.astype(BF)


ROLES = (4, 3, 1, -3, -1, 2, -2, 0)


def on_device(expert_ids, grad_hidden, stored_inputs, gate_weight, up_weight):
    peers = lax.axis_size("expert")
    replicas = lax.axis_size("dp")
    chips = replicas // 2
    cap, width = stored_inputs.shape[3], stored_inputs.shape[4]
    hidden = gate_weight.shape[2]
    tokens, picks = expert_ids.shape
    routed, slot_rows = tokens * picks, peers * cap
    sds = jax.ShapeDtypeStruct
    w_gate, w_up = gate_weight[0], up_weight[0]
    x = stored_inputs[0, 0].transpose(1, 0, 2).reshape(slot_rows, width)
    spot = lax.axis_index("dp")
    spot = jnp.stack([spot % 2, spot // 2]).astype(jnp.int32)

    def along_z(value, offset):
        pairs = []
        for z in range(chips):
            for core in range(2):
                to = (z + (offset if core == 0 else -offset)) % chips
                pairs.append((2 * z + core, 2 * to + core))
        return lax.ppermute(value, "dp", pairs)

    swap = functools.partial(lax.ppermute, axis_name="dp", perm=[(i, i ^ 1) for i in range(replicas)])

    in_rows = -(-(cap * hidden // LANES) // 8) * 8
    outgoing, take = call(
        functools.partial(pack, peers, cap),
        (sds((peers * in_rows, LANES), BF), sds((tokens, slot_rows), BF)),
        "hh",
        [pltpu.VMEM((peers * in_rows, LANES), F32)],
        flops=2 * slot_rows * routed * hidden,
        moved=4 * peers * in_rows * LANES,
    )(expert_ids.T, grad_hidden.reshape(routed, hidden))
    arrived = lax.all_to_all(outgoing.reshape(peers, in_rows, LANES), "expert", 0, 0, tiled=True)

    half = chips * LANES
    lent = call(partner_columns, sds((slot_rows, half), BF), "sh", moved=4 * slot_rows * half)(spot, x)
    borrowed = swap(lent)
    parts = hidden // 256
    f_gate, f_up = pl.pallas_call(
        factors,
        grid=(parts,),
        out_shape=(sds((slot_rows, hidden), F32),) * 2,
        in_specs=[
            pl.BlockSpec((slot_rows, width), lambda i: (0, 0)),
            pl.BlockSpec((width, 256), lambda i: (0, i)),
            pl.BlockSpec((width, 256), lambda i: (0, i)),
        ],
        out_specs=(pl.BlockSpec((slot_rows, 256), lambda i: (0, i)),) * 2,
        compiler_params=pltpu.CompilerParams(vmem_limit_bytes=24 * MIB),
        cost_estimate=pl.CostEstimate(
            flops=4 * slot_rows * width * hidden, bytes_accessed=8 * width * hidden, transcendentals=slot_rows * hidden
        ),
    )(far(x), far(w_gate), far(w_up))
    apart = -(-slot_rows // LANES) * LANES
    x_roles = call(
        functools.partial(by_role, ROLES),
        sds((len(ROLES) * LANES, 2 * apart), BF),
        "shv",
        moved=8 * slot_rows * half,
        near=True,
    )(spot, x, borrowed)

    dgate, dup = call(
        functools.partial(hidden_grads, peers, cap),
        (sds((slot_rows, hidden), BF),) * 2,
        "dddo",
        [pltpu.VMEM((peers * in_rows, LANES), F32)],
        moved=16 * slot_rows * hidden,
        near=True,
    )(arrived.reshape(peers * in_rows, LANES), f_gate, f_up, x_roles)
    dgate_near = swap(dgate)

    out_rows, steps = cap * width // LANES, 4
    back = call(
        functools.partial(input_grads, peers, cap),
        sds((peers * out_rows, LANES), BF),
        "vvuu",
        [
            pltpu.VMEM((peers * out_rows, LANES), F32),
            pltpu.VMEM((steps, width // steps, hidden), BF),
            pltpu.VMEM((steps, width // steps, hidden), BF),
            pltpu.SemaphoreType.DMA((2, steps)),
        ],
        flops=1,
        moved=1,
    )(dgate, dup, w_gate, w_up)
    blocks = [sds((n * LANES, hidden), BF) for n in (1, 2, 2, 3)]
    most, right, left, kept, back = call(
        partials,
        blocks + [pltpu.HBM(back.shape, BF)],
        "vvvu",
        flops=1,
        moved=1,
        near=True,
        alias={3: len(blocks)},
    )(x_roles, dgate, dgate_near, back)
    returned = lax.all_to_all(back.reshape(peers, out_rows, LANES), "expert", 0, 0, tiled=True)

    most_in = along_z(most, 2)
    right_in = along_z(right, 1)
    left_in = along_z(left, -1)

    moved = 10 * LANES * hidden
    block = sds((LANES, hidden), BF)
    part = call(sum_most, sds((LANES, hidden), F32), "vv", flops=5_000_000_000, moved=moved, near=True)(kept, most_in)
    right_sum = call(sum_right, block, "vv", flops=10_500_000_000, moved=moved, near=True)(part, right_in)
    left_sum = call(sum_left, block, "vv", flops=1, moved=moved, near=True)(kept, left_in)
    right_sum = along_z(right_sum, 2)
    left_sum = along_z(left_sum, -2)
    grad_tokens = call(
        functools.partial(combine, peers, cap),
        sds((tokens, width), BF),
        "vv",
        [pltpu.VMEM((peers * out_rows, LANES), F32)],
        flops=1,
        moved=1,
    )(take, returned.reshape(peers * out_rows, LANES))
    grad_gate = call(sum_own, sds((LANES, hidden), F32), "vvvvvu", moved=2 * moved)(
        kept, right_in, left_in, right_sum, left_sum, grad_tokens
    )
    return (grad_tokens, grad_gate[None])


def solution(mesh):
    return jax.shard_map(
        on_device,
        mesh=mesh,
        in_specs=(
            P(("dp", "expert"), None),
            P(("dp", "expert"), None, None),
            P("dp", "expert", None, None, None),
            P("expert", None, None),
            P("expert", None, None),
        ),
        out_specs=(P(("dp", "expert"), None), P("expert", "dp", None)),
        check_vma=False,
    )
```

```python
import functools

import jax
import jax.numpy as jnp
from jax import lax
from jax.experimental import pallas as pl
from jax.experimental.pallas import tpu as pltpu
from jax.sharding import PartitionSpec as P

BF, F32 = jnp.bfloat16, jnp.float32
LANES = 128
MIB = 1 << 20
AHEAD = 2
NT = (((1,), (1,)), ((), ()))


def call(body, outs, ins, scratch=(), flops=0, moved=0, near=False, alias=None, vmem=16):
    specs = {"h": pl.BlockSpec(), "d": pl.BlockSpec(), "v": pl.BlockSpec(memory_space=pltpu.VMEM)}
    specs |= {"s": pl.BlockSpec(memory_space=pltpu.SMEM), "u": pl.BlockSpec(memory_space=pl.ANY), "o": pl.BlockSpec(memory_space=pl.ANY)}
    out_specs = jax.tree.map(lambda _: specs["v" if near else "h"], outs)
    if alias:
        ((source, place),) = alias.items()
        out_specs[place] = specs[ins[source]]
    kernel = pl.pallas_call(
        body,
        out_shape=outs if near else jax.tree.map(lambda out: pltpu.HBM(out.shape, out.dtype), outs),
        in_specs=[specs[kind] for kind in ins],
        out_specs=out_specs,
        input_output_aliases=alias or {},
        scratch_shapes=list(scratch),
        compiler_params=pltpu.CompilerParams(vmem_limit_bytes=vmem * MIB),
        cost_estimate=pl.CostEstimate(flops=flops, bytes_accessed=moved, transcendentals=0),
    )
    return lambda *given: kernel(*(far(v) if kind in "hu" else v for kind, v in zip(ins, given)))


def far(value):
    return pltpu.with_memory_space_constraint(value, pltpu.HBM)


def iota(shape, axis):
    return lax.broadcasted_iota(jnp.int32, shape, axis)


def pack(peers, cap, ids_ref, grads_ref, out_ref, take_ref, wide_ref):
    picks, tokens = ids_ref.shape
    routed, hidden = grads_ref.shape
    ids = ids_ref[...].astype(F32).astype(BF)
    token_of = (iota((tokens, routed), 1) // picks == iota((tokens, routed), 0)).astype(F32).astype(BF)
    by_row = jnp.dot(ids, token_of, preferred_element_type=F32)
    mine = iota((picks, routed), 1) % picks == iota((picks, routed), 0)
    e_row = jnp.sum(jnp.where(mine, by_row, 0.0), axis=0, keepdims=True)
    token_col = (iota((routed, tokens), 0) // picks == iota((routed, tokens), 1)).astype(F32).astype(BF)
    by_col = lax.dot_general(token_col, ids, NT, preferred_element_type=F32)
    mine = iota((routed, picks), 0) % picks == iota((routed, picks), 1)
    e_col = jnp.sum(jnp.where(mine, by_col, 0.0), axis=1, keepdims=True)
    earlier = iota((routed, routed), 0) < iota((routed, routed), 1)
    slot = jnp.sum(jnp.where(earlier & (e_col == e_row), 1.0, 0.0), axis=0, keepdims=True)
    row = slot * peers + e_row
    place = (iota((cap * peers, routed), 0).astype(F32) == row).astype(F32).astype(BF)
    sent = jnp.dot(place, grads_ref[...], preferred_element_type=F32)
    cols = hidden // LANES
    rows = wide_ref.shape[0] // peers
    for j in range(cap):
        for c in range(cols):
            wide_ref[pl.ds(j * cols + c, peers, stride=rows), :] = sent[
                j * peers : (j + 1) * peers, c * LANES : (c + 1) * LANES
            ]
    out_ref[...] = wide_ref[...].astype(BF)
    take_ref[...] = lax.dot_general(token_of, place, NT, preferred_element_type=F32).astype(BF)


def partner_columns(core_ref, x_ref, out_ref):
    other = 1 - core_ref[0]
    for z in range(out_ref.shape[1] // LANES):
        start = pl.multiple_of((2 * z + other) * LANES, LANES)
        out_ref[:, z * LANES : (z + 1) * LANES] = x_ref[:, pl.ds(start, LANES)]


def by_role(roles, spot_ref, x_ref, partner_ref, out_ref):
    core, z = spot_ref[0], spot_ref[1]
    chips = partner_ref.shape[1] // LANES
    rows, apart = x_ref.shape[0], out_ref.shape[1] // 2
    sign = 1 - 2 * core
    for n, offset in zip(range(0, out_ref.shape[0], LANES), roles):
        chip = lax.rem(z + sign * offset + chips, chips)
        start = pl.multiple_of((2 * chip + core) * LANES, LANES)
        own = x_ref[:, pl.ds(start, LANES)].astype(F32)
        near = partner_ref[:, pl.ds(pl.multiple_of(chip * LANES, LANES), LANES)].astype(F32)
        out_ref[n : n + LANES, :rows] = own.T.astype(BF)
        out_ref[n : n + LANES, apart : apart + rows] = near.T.astype(BF)


def factors(x_ref, wg_ref, wu_ref, fg_ref, fu_ref):
    x = x_ref[...]
    gate = jnp.dot(x, wg_ref[...], preferred_element_type=F32)
    up = jnp.dot(x, wu_ref[...], preferred_element_type=F32)
    sig = 1.0 / (1.0 + jnp.exp(-gate))
    fg_ref[...] = up * sig * (1.0 + gate * (1.0 - sig))
    fu_ref[...] = gate * sig


def hidden_grads(peers, cap, got_ref, fg_ref, fu_ref, _, dgate_ref, dup_ref, wide_ref):
    wide_ref[...] = got_ref[...].astype(F32)
    rows = wide_ref.shape[0] // peers
    cols = fg_ref.shape[1] // LANES
    for j in range(cap):
        for c in range(cols):
            at = (slice(j * peers, (j + 1) * peers), slice(c * LANES, (c + 1) * LANES))
            piece = wide_ref[pl.ds(j * cols + c, peers, stride=rows), :]
            dgate_ref[at] = (piece * fg_ref[at]).astype(BF)
            dup_ref[at] = (piece * fu_ref[at]).astype(BF)


def input_grads(peers, cap, *refs):
    dgate_ref, dup_ref, wg_hbm, wu_hbm, out_ref, wide_ref, wg_ref, wu_ref, sems = refs
    steps, width, _ = wg_ref.shape
    copies = [
        [
            pltpu.make_async_copy(source.at[pl.ds(n * width, width)], held.at[n], sems.at[i, n])
            for i, (source, held) in enumerate(((wg_hbm, wg_ref), (wu_hbm, wu_ref)))
        ]
        for n in range(steps)
    ]
    for pair in copies[:AHEAD]:
        for copy in pair:
            copy.start()
    rows = wide_ref.shape[0] // peers
    cols = width // LANES
    for n in range(steps):
        for copy in copies[n]:
            copy.wait()
        for copy in copies[n + AHEAD] if n + AHEAD < steps else ():
            copy.start()
        back = lax.dot_general(dgate_ref[...], wg_ref[n], NT, preferred_element_type=F32)
        back = back + lax.dot_general(dup_ref[...], wu_ref[n], NT, preferred_element_type=F32)
        for j in range(cap):
            for c in range(cols):
                at = pl.ds(j * (rows // cap) + n * cols + c, peers, stride=rows)
                wide_ref[at, :] = back[j * peers : (j + 1) * peers, c * LANES : (c + 1) * LANES]
    out_ref[...] = wide_ref[...].astype(BF)


def partials(xt_ref, own_ref, near_ref, _, *refs):
    *outs, _ = refs
    rows, apart = own_ref.shape[0], xt_ref.shape[1] // 2
    first = 0
    for out in outs:
        part = slice(first, first + out.shape[0])
        total = jnp.dot(xt_ref[part, :rows], own_ref[...], preferred_element_type=F32)
        total = total + jnp.dot(xt_ref[part, apart : apart + rows], near_ref[...], preferred_element_type=F32)
        out[...] = total.astype(BF)
        first += out.shape[0]


def sum_most(kept_ref, most_ref, out_ref):
    out_ref[...] = kept_ref[:LANES].astype(F32) + most_ref[...].astype(F32)


def sum_right(part_ref, right_ref, out_ref):
    out_ref[...] = (part_ref[...] + right_ref[...].astype(F32)).astype(BF)


def sum_left(kept_ref, left_ref, out_ref):
    out_ref[...] = (kept_ref[LANES : 2 * LANES].astype(F32) + left_ref[:LANES].astype(F32)).astype(BF)


def sum_own(kept_ref, right_ref, left_ref, right_sum_ref, left_sum_ref, _, out_ref):
    near_sum = right_ref[...].astype(F32) + left_ref[LANES:].astype(F32)
    far_sum = right_sum_ref[...].astype(F32) + left_sum_ref[...].astype(F32)
    out_ref[...] = kept_ref[2 * LANES :].astype(F32) + near_sum + far_sum


def combine(peers, cap, take_ref, got_ref, out_ref, wide_ref):
    wide_ref[...] = got_ref[...].astype(F32)
    rows = wide_ref.shape[0] // peers
    cols = rows // cap
    for c in range(cols):
        part = [wide_ref[pl.ds(j * cols + c, peers, stride=rows), :] for j in range(cap)]
        piece = jnp.concatenate(part, axis=0).astype(BF)
        total = jnp.dot(take_ref[...], piece, preferred_element_type=F32)
        out_ref[:, c * LANES : (c + 1) * LANES] = total.astype(BF)


ROLES = (4, 3, -3, -1, 1, 2, -2, 0)


def on_device(expert_ids, grad_hidden, stored_inputs, gate_weight, up_weight):
    peers = lax.axis_size("expert")
    replicas = lax.axis_size("dp")
    chips = replicas // 2
    cap, width = stored_inputs.shape[3], stored_inputs.shape[4]
    hidden = gate_weight.shape[2]
    tokens, picks = expert_ids.shape
    routed, slot_rows = tokens * picks, peers * cap
    sds = jax.ShapeDtypeStruct
    w_gate, w_up = gate_weight[0], up_weight[0]
    x = stored_inputs[0, 0].transpose(1, 0, 2).reshape(slot_rows, width)
    spot = lax.axis_index("dp")
    spot = jnp.stack([spot % 2, spot // 2]).astype(jnp.int32)

    def along_z(value, offset):
        pairs = []
        for z in range(chips):
            for core in range(2):
                to = (z + (offset if core == 0 else -offset)) % chips
                pairs.append((2 * z + core, 2 * to + core))
        return lax.ppermute(value, "dp", pairs)

    swap = functools.partial(lax.ppermute, axis_name="dp", perm=[(i, i ^ 1) for i in range(replicas)])

    in_rows = -(-(cap * hidden // LANES) // 8) * 8
    outgoing, take = call(
        functools.partial(pack, peers, cap),
        (sds((peers * in_rows, LANES), BF), sds((tokens, slot_rows), BF)),
        "hh",
        [pltpu.VMEM((peers * in_rows, LANES), F32)],
        flops=2 * slot_rows * routed * hidden,
        moved=4 * peers * in_rows * LANES,
    )(expert_ids.T, grad_hidden.reshape(routed, hidden))
    arrived = lax.all_to_all(outgoing.reshape(peers, in_rows, LANES), "expert", 0, 0, tiled=True)

    half = chips * LANES
    lent = call(partner_columns, sds((slot_rows, half), BF), "sh", moved=4 * slot_rows * half)(spot, x)
    borrowed = swap(lent)
    parts = hidden // 256
    f_gate, f_up = pl.pallas_call(
        factors,
        grid=(parts,),
        out_shape=(sds((slot_rows, hidden), F32),) * 2,
        in_specs=[
            pl.BlockSpec((slot_rows, width), lambda i: (0, 0)),
            pl.BlockSpec((width, 256), lambda i: (0, i)),
            pl.BlockSpec((width, 256), lambda i: (0, i)),
        ],
        out_specs=(pl.BlockSpec((slot_rows, 256), lambda i: (0, i)),) * 2,
        compiler_params=pltpu.CompilerParams(vmem_limit_bytes=24 * MIB),
        cost_estimate=pl.CostEstimate(
            flops=4 * slot_rows * width * hidden, bytes_accessed=8 * width * hidden, transcendentals=slot_rows * hidden
        ),
    )(far(x), far(w_gate), far(w_up))
    apart = -(-slot_rows // LANES) * LANES
    x_roles = call(
        functools.partial(by_role, ROLES),
        sds((len(ROLES) * LANES, 2 * apart), BF),
        "shv",
        moved=8 * slot_rows * half,
        near=True,
    )(spot, x, borrowed)

    dgate, dup = call(
        functools.partial(hidden_grads, peers, cap),
        (sds((slot_rows, hidden), BF),) * 2,
        "dddo",
        [pltpu.VMEM((peers * in_rows, LANES), F32)],
        moved=16 * slot_rows * hidden,
        near=True,
    )(arrived.reshape(peers * in_rows, LANES), f_gate, f_up, x_roles)
    dgate_near = swap(dgate)

    out_rows, steps = cap * width // LANES, 4
    back = call(
        functools.partial(input_grads, peers, cap),
        sds((peers * out_rows, LANES), BF),
        "vvuu",
        [
            pltpu.VMEM((peers * out_rows, LANES), F32),
            pltpu.VMEM((steps, width // steps, hidden), BF),
            pltpu.VMEM((steps, width // steps, hidden), BF),
            pltpu.SemaphoreType.DMA((2, steps)),
        ],
        flops=1,
        moved=1,
    )(dgate, dup, w_gate, w_up)
    blocks = [sds((n * LANES, hidden), BF) for n in (1, 1, 2, 1, 3)]
    most, right, left, right_own, kept, back = call(
        partials,
        blocks + [pltpu.HBM(back.shape, BF)],
        "vvvu",
        flops=1,
        moved=1,
        near=True,
        alias={3: len(blocks)},
    )(x_roles, dgate, dgate_near, back)
    returned = lax.all_to_all(back.reshape(peers, out_rows, LANES), "expert", 0, 0, tiled=True)

    most_in = along_z(most, 2)
    right_in = along_z(right, 1)
    left_in = along_z(left, -1)
    right_own_in = along_z(right_own, 1)

    moved = 10 * LANES * hidden
    block = sds((LANES, hidden), BF)
    part = call(sum_most, sds((LANES, hidden), F32), "vv", flops=5_000_000_000, moved=moved, near=True)(kept, most_in)
    right_sum = call(sum_right, block, "vv", flops=10_500_000_000, moved=moved, near=True)(part, right_in)
    left_sum = call(sum_left, block, "vv", flops=1, moved=moved, near=True)(kept, left_in)
    right_sum = along_z(right_sum, 2)
    left_sum = along_z(left_sum, -2)
    grad_tokens = call(
        functools.partial(combine, peers, cap),
        sds((tokens, width), BF),
        "vv",
        [pltpu.VMEM((peers * out_rows, LANES), F32)],
        flops=1,
        moved=1,
    )(take, returned.reshape(peers * out_rows, LANES))
    grad_gate = call(sum_own, sds((LANES, hidden), F32), "vvvvvu", moved=2 * moved)(
        kept, right_own_in, left_in, right_sum, left_sum, grad_tokens
    )
    return (grad_tokens, grad_gate[None])


def solution(mesh):
    return jax.shard_map(
        on_device,
        mesh=mesh,
        in_specs=(
            P(("dp", "expert"), None),
            P(("dp", "expert"), None, None),
            P("dp", "expert", None, None, None),
            P("expert", None, None),
            P("expert", None, None),
        ),
        out_specs=(P(("dp", "expert"), None), P("expert", "dp", None)),
        check_vma=False,
    )
```
